256 devices in a mesh: dp: 16 (over x_lo, z), fsdp: 16 (over x_hi, y, core).
Axes of the slice: x: 4 (x_hi: 2, x_lo: 2; x = x_hi * 2 + x_lo), y: 4, z: 8, core: 2. Of those that a mesh axis runs over, the one named last changes fastest.
Arguments:
- hidden: bfloat16 [32, 1536, 5120], P('dp', 'fsdp'), may hold values from -6 to 6
- w_qkv: bfloat16 [5120, 1280], P('fsdp'), may hold values from -0.078125 to 0.078125
- norm_gains: float32 [2, 128], replicated, may hold values from 0.5 to 1.5
- upstream: bfloat16 [32, 1536, 1024], P('dp', 'fsdp'), may hold values from -12 to 12
- segment_ids: int32 [32, 1536], P('dp', 'fsdp'), may hold values from 0 to 8, as said below
- advantages: bfloat16 [32, 8], P('dp'), may hold values from -4 to 4
- swap_slot: int32 [8], replicated, may hold values from 0 to 1, as said below
- token_count: int32 [1], replicated, may hold values from 12288 to 49152
Outputs:
- grad_hidden: bfloat16 [32, 1536, 5120], P('dp', 'fsdp')
- grad_weight: float32 [16, 5120, 1280], P('dp', 'fsdp')
- grad_gains: float32 [16, 2, 128], P('dp')
The draws below stay inside these ranges and needn't reach their ends.
Inputs may be any that keep to these rules, and one draw needn't show every extreme that they name: `segment_ids`: along a pack the ids never fall; id 8 marks padding, which closes every pack; a pack of data rank r uses ids 0 to 7 * r // 15 at most for responses. `swap_slot`: entry q is the slot exchanged by data ranks q and 15 - q; consecutive entries differ.
All inputs are finite; a program needn't handle non-finite values.
Results may differ from the reference program's by a relative error of at most 0.022.
Values may be sent and summed in bfloat16 or wider, within the bound.
No kernel may reach another device: no remote copies, remote signals or barrier semaphores. Data moves between devices by JAX's collectives and lax.ppermute only.
A program may use at most 128 MiB of HBM per device.

```python
import math
import jax
import jax.numpy as jnp
from jax import lax

D = 5120
HD = 128
QPER = 8
GROUPS = 1
SEGS = 8
PACKS = 2
SLICE = 96
SEQ = 1536
NPACK = 32
ALLTOK = 49152
QW = 1024
COLS = 1280
N_DP = 16
N_FSDP = 16


def draw_segment_ids(key, part):
    key = jax.random.fold_in(key, 7)
    pad_key, cut_key = jax.random.split(key)
    data_rank = jnp.arange(NPACK, dtype=jnp.int32) // PACKS
    responses = 1 + (SEGS - 1) * data_rank // max(N_DP - 1, 1)
    padding = 1 + jax.random.randint(pad_key, (NPACK,), 0, max(SEQ // 4, 1))
    filled = SEQ - padding
    drawn = jax.random.randint(cut_key, (NPACK, SEGS - 1), 0, 1 << 20)
    cuts = 1 + drawn % jnp.maximum(filled - 1, 1)[:, None]
    active = jnp.arange(SEGS - 1, dtype=jnp.int32)[None, :] < (responses - 1)[:, None]
    cuts = jnp.where(active, cuts, SEQ + 1)
    place = jnp.arange(SEQ, dtype=jnp.int32)
    numbers = jnp.sum((cuts[:, :, None] <= place[None, None, :]).astype(jnp.int32), 1)
    return jnp.where(place[None, :] >= filled[:, None], SEGS, numbers).astype(jnp.int32)


def draw_swap_slot(key, part):
    key = jax.random.fold_in(key, 11)
    start_key, step_key = jax.random.split(key)
    first = jax.random.randint(start_key, (1,), 0, PACKS)
    steps = jax.random.randint(step_key, (N_DP // 2,), 1, max(PACKS, 2))
    steps = jnp.where(jnp.arange(N_DP // 2, dtype=jnp.int32) == 0, 0, steps)
    return ((first + jnp.cumsum(steps)) % PACKS).astype(jnp.int32)


def spiked(values, key, source, target, blocks, factor):
    owner, partner = [(jnp.arange(values.shape[position]) // (values.shape[position] // blocks)).reshape([-1 if axis == position else 1 for axis in range(values.ndim)]) for position in (source, target)]
    chosen = jax.random.permutation(key, blocks)[partner]
    strong = (owner == chosen) | (owner == (partner + blocks // 2) % blocks)
    return jnp.where(strong, factor * values, values)


def levels(key, dims, cuts, low, largest):
    loudness = 1.0
    for position, blocks in cuts:
        heights = jax.random.uniform(jax.random.fold_in(jax.random.fold_in(key, 6), position), (blocks,), jnp.float32, low / len(cuts), largest / len(cuts))
        loudness = loudness * jnp.repeat(jnp.exp(heights), dims[position] // blocks).reshape((-1,) + (1,) * (len(dims) - 1 - position))
    return loudness


def normal_values(own_key, shape, deviation, most, pieces=(), held_as=jnp.bfloat16):
    factor_of = levels(own_key, shape, pieces, -0.22, 0.18) if pieces else 1.0
    entries = jax.random.normal(own_key, shape, jnp.float32) * deviation * factor_of
    return jnp.minimum(jnp.maximum(entries, -most), most).astype(held_as)


def gaussian_with(stream_key, dims, width, most, cuts, heavy, kind=jnp.bfloat16):
    values = width * jax.random.normal(stream_key, dims, jnp.float32)
    if cuts:
        values = values * levels(stream_key, dims, cuts, -0.22, 0.18)
    return jnp.clip(spiked(values, jax.random.fold_in(stream_key, 3), *heavy), -most, most).astype(kind)


def setup_inputs(seed: int = 0) -> dict:
    keys = jax.random.split(jax.random.key(seed), 9)
    hidden = gaussian_with(keys[0], (NPACK, SEQ, D), 1.0, 6.0, ((0, 16), (1, 16)), (1, 2, 16, 2.0))
    w_qkv = normal_values(keys[1], (D, COLS), D ** -0.5, 0.078125, ((0, 16),))
    norm_gains = jnp.clip(1.0 + 0.1 * jax.random.normal(keys[2], (2, HD), jnp.float32), 0.5, 1.5)
    upstream = normal_values(keys[3], (NPACK, SEQ, QW), 2.0, 12.0, ((0, 16), (1, 16)))
    segment_ids = draw_segment_ids(jax.random.fold_in(keys[8], 71), 0)
    advantages = normal_values(keys[5], (NPACK, SEGS), 1.0, 4.0, ((0, 16),))
    swap_slot = draw_swap_slot(jax.random.fold_in(keys[8], 71), 0)
    token_count = jax.random.randint(keys[7], (1,), ALLTOK // 4, ALLTOK + 1).astype(jnp.int32)
    return dict(hidden=hidden, w_qkv=w_qkv, norm_gains=norm_gains, upstream=upstream, segment_ids=segment_ids, advantages=advantages, swap_slot=swap_slot, token_count=token_count)


EPSILON = 1e-06
THETA_LOG = math.log(1000000.0)

def rope_tables(positions, head_size):
    half_size = head_size // 2
    inverse = jnp.exp(-(jnp.arange(half_size, dtype=jnp.float32) * (2.0 / head_size)) * THETA_LOG)
    angles = positions.astype(jnp.float32)[..., None] * inverse
    return (jnp.cos(angles), jnp.sin(angles))

def rotate(vector, cosine, sine_part):
    half_size = vector.shape[-1] // 2
    leading = vector[..., :half_size]
    trailing = vector[..., half_size:]
    return jnp.concatenate([leading * cosine - trailing * sine_part, trailing * cosine + leading * sine_part], -1)

def unrotate(gradient, cosine, sine_part):
    half_size = gradient.shape[-1] // 2
    leading = gradient[..., :half_size]
    trailing = gradient[..., half_size:]
    return jnp.concatenate([leading * cosine + trailing * sine_part, trailing * cosine - leading * sine_part], -1)

def normalize(vector, gain_row):
    inverse_rms = lax.rsqrt(lax.optimization_barrier(jnp.mean(vector * vector, -1, keepdims=True)) + EPSILON)
    return (vector * inverse_rms * gain_row, inverse_rms)

def normalize_grad(vector, inverse_rms, gain_row, gradient):
    weighted = gradient * gain_row
    inner = lax.optimization_barrier(jnp.mean(vector * weighted, -1, keepdims=True))
    grad_in = inverse_rms * weighted - vector * (inverse_rms * inverse_rms * inverse_rms) * inner
    gain_terms = gradient * (vector * inverse_rms)
    return (grad_in, gain_terms)

def attend(queries, key_rows, value_rows, allowed, cotangent, head_size):
    scaling = 1.0 / math.sqrt(head_size)
    queries_f = queries.astype(jnp.float32)
    keys_f = key_rows.astype(jnp.float32)
    values_f = value_rows.astype(jnp.float32)
    cotangent_f = cotangent.astype(jnp.float32)
    scores = jnp.einsum('sgqd,ugd->gqsu', queries_f, keys_f) * scaling
    exps = jnp.where(allowed[None, None], jnp.exp(scores), 0.0)
    probabilities = exps / lax.optimization_barrier(jnp.sum(exps, -1, keepdims=True))
    probs_b = probabilities.astype(jnp.bfloat16).astype(jnp.float32)
    attended = jnp.einsum('gqsu,ugd->sgqd', probs_b, values_f)
    grad_values = jnp.einsum('gqsu,sgqd->ugd', probs_b, cotangent_f)
    grad_probs = jnp.einsum('sgqd,ugd->gqsu', cotangent_f, values_f)
    row_terms = jnp.einsum('sgqd,sgqd->gqs', cotangent_f, attended)
    grad_scores = (probabilities * (grad_probs - row_terms[..., None]) * scaling).astype(jnp.bfloat16).astype(jnp.float32)
    grad_queries = jnp.einsum('gqsu,ugd->sgqd', grad_scores, keys_f)
    grad_keys = jnp.einsum('gqsu,sgqd->ugd', grad_scores, queries_f)
    return (grad_queries, grad_keys, grad_values)

def reference(hidden, w_qkv, norm_gains, upstream, segment_ids, advantages, swap_slot, token_count):
    pack_total, seq_len, model_width = hidden.shape
    query_width = GROUPS * QPER * HD
    kv_width = GROUPS * HD
    permuted = jnp.arange(pack_total, dtype=jnp.int32)
    for pair_index in range(N_DP // 2):
        pack_slot = swap_slot[pair_index]
        low_pack = pair_index * PACKS + pack_slot
        high_pack = (N_DP - 1 - pair_index) * PACKS + pack_slot
        permuted = permuted.at[low_pack].set(high_pack).at[high_pack].set(low_pack)
    hidden_b = hidden[permuted]
    upstream_b = upstream[permuted]
    segments_b = segment_ids[permuted]
    advantage_b = advantages[permuted]
    place = jnp.arange(seq_len, dtype=jnp.int32)
    starts = lax.optimization_barrier(jnp.sum((segments_b[:, None, :] < segments_b[:, :, None]).astype(jnp.int32), -1))
    positions = place[None, :] - starts
    projected = jnp.dot(hidden_b.reshape(-1, model_width), w_qkv, preferred_element_type=jnp.float32)
    projected = projected.reshape(pack_total, seq_len, COLS)
    queries = projected[..., :query_width].reshape(pack_total, seq_len, GROUPS, QPER, HD)
    key_part = projected[..., query_width:query_width + kv_width].reshape(pack_total, seq_len, GROUPS, HD)
    value_part = projected[..., query_width + kv_width:].reshape(pack_total, seq_len, GROUPS, HD)
    queries_n, query_rms = normalize(queries, norm_gains[0])
    keys_n, key_rms = normalize(key_part, norm_gains[1])
    cosine, sine_part = rope_tables(positions, HD)
    cos_query = cosine[:, :, None, None, :]
    sin_query = sine_part[:, :, None, None, :]
    cos_key = cosine[:, :, None, :]
    sin_key = sine_part[:, :, None, :]
    queries_r = rotate(queries_n, cos_query, sin_query).astype(jnp.bfloat16)
    keys_r = rotate(keys_n, cos_key, sin_key).astype(jnp.bfloat16)
    values_b = value_part.astype(jnp.bfloat16)
    segment_table = (segments_b[..., None] == jnp.arange(SEGS, dtype=jnp.int32)).astype(jnp.float32)
    per_token = lax.optimization_barrier(jnp.sum(segment_table * advantage_b.astype(jnp.float32)[:, None, :], -1))
    factor = jnp.float32(ALLTOK) / token_count[0].astype(jnp.float32)
    cotangent = (upstream_b.astype(jnp.float32) * (per_token * factor)[..., None]).astype(jnp.bfloat16)
    cotangent = cotangent.reshape(pack_total, seq_len, GROUPS, QPER, HD)

    def one_pack(items):
        queries_p, keys_p, values_p, segments_p, cotangent_p = items
        allowed = (segments_p[:, None] == segments_p[None, :]) & (place[:, None] >= place[None, :])
        query_blocks = queries_p.reshape(N_FSDP, SLICE, GROUPS, QPER, HD)
        allowed_blocks = allowed.reshape(N_FSDP, SLICE, seq_len)
        cotangent_blocks = cotangent_p.reshape(N_FSDP, SLICE, GROUPS, QPER, HD)

        def one_block(block_items):
            grad_queries, grad_keys, grad_values = attend(block_items[0], keys_p, values_p, block_items[1], block_items[2], HD)
            joined = jnp.concatenate([grad_keys.reshape(seq_len, kv_width), grad_values.reshape(seq_len, kv_width)], -1)
            return (grad_queries, joined.astype(jnp.bfloat16))
        grad_queries, joined = lax.map(one_block, (query_blocks, allowed_blocks, cotangent_blocks))
        joined = lax.optimization_barrier(joined)
        summed = lax.optimization_barrier(jnp.sum(joined.astype(jnp.float32), 0))
        return (grad_queries.reshape(seq_len, GROUPS, QPER, HD), summed)
    grad_queries_r, key_value_grad = lax.map(one_pack, (queries_r, keys_r, values_b, segments_b, cotangent))
    grad_keys_r = key_value_grad[..., :kv_width].reshape(pack_total, seq_len, GROUPS, HD)
    grad_values = key_value_grad[..., kv_width:]
    grad_queries_n = unrotate(grad_queries_r, cos_query, sin_query)
    grad_keys_n = unrotate(grad_keys_r, cos_key, sin_key)
    grad_queries, query_gain_terms = normalize_grad(queries, query_rms, norm_gains[0], grad_queries_n)
    grad_keys, key_gain_terms = normalize_grad(key_part, key_rms, norm_gains[1], grad_keys_n)
    grad_projected = jnp.concatenate([grad_queries.reshape(pack_total, seq_len, query_width), grad_keys.reshape(pack_total, seq_len, kv_width), grad_values], -1).astype(jnp.bfloat16)
    grad_hidden = jnp.dot(grad_projected.reshape(-1, COLS), w_qkv.T, preferred_element_type=jnp.float32)
    grad_hidden = grad_hidden.astype(jnp.bfloat16).reshape(pack_total, seq_len, model_width)
    query_gain = lax.optimization_barrier(jnp.sum(query_gain_terms.reshape(N_DP, -1, HD), 1))
    key_gain = lax.optimization_barrier(jnp.sum(key_gain_terms.reshape(N_DP, -1, HD), 1))
    grad_gains = jnp.stack([query_gain, key_gain], 1)
    hidden_parts = hidden_b.reshape(N_DP, PACKS, N_FSDP, SLICE, model_width).transpose(0, 2, 1, 3, 4).reshape(N_DP, N_FSDP, PACKS * SLICE, model_width)
    grad_parts = grad_projected.reshape(N_DP, PACKS, N_FSDP, SLICE, COLS).transpose(0, 2, 1, 3, 4).reshape(N_DP, N_FSDP, PACKS * SLICE, COLS)

    def one_rank(rank_items):

        def add_device(totals, device_items):
            partial_value = lax.dot_general(device_items[0], device_items[1], (((0,), (0,)), ((), ())), preferred_element_type=jnp.float32)
            rounded = lax.optimization_barrier(partial_value.astype(jnp.bfloat16))
            return (totals + rounded.astype(jnp.float32), None)
        totals, unused = lax.scan(add_device, jnp.zeros((model_width, COLS), jnp.float32), rank_items)
        return totals
    grad_weight = lax.map(one_rank, (hidden_parts, grad_parts))
    return (grad_hidden, grad_weight, grad_gains)
```

```python
import math

import jax
import jax.numpy as jnp
from jax import lax
from jax.experimental import pallas as pl
from jax.experimental.pallas import tpu as pltpu
from jax.sharding import PartitionSpec as P

HD = 128
HEADS = 4
TOK = 96
CHIPS = 8
UNIT = 640
HALF_COLS = 640
QCOLS = HEADS * HD
SEQ = 1536
SEGS = 8
EPSILON = 1e-06
THETA_LOG = math.log(1000000.0)
SCALING = 1.0 / math.sqrt(HD)
EXP2_SCALE = SCALING * math.log2(math.e)
F32 = jnp.float32
BF16 = jnp.bfloat16
NN = (((1,), (0,)), ((), ()))
NT = (((1,), (1,)), ((), ()))
TN = (((0,), (0,)), ((), ()))
VMEM_LIMIT = 56 * 1024 * 1024


def core_mate(array):
    return lax.ppermute(array, "fsdp", [(i, i ^ 1) for i in range(16)])


def from_y(array, step):
    def there(i):
        return (i & 8) | (((i // 2 - step) % 4) * 2) | (i & 1)

    return lax.ppermute(array, "fsdp", [(i, there(i)) for i in range(16)])


def from_x(array):
    return lax.ppermute(array, "fsdp", [(i, i ^ 8) for i in range(16)])


def from_near_x(array):
    pairs = [(d * 16 + i, (d ^ 8) * 16 + (i ^ 8)) for d in range(16) for i in range(16)]
    return lax.ppermute(array, ("dp", "fsdp"), pairs)


def mirror(array):
    return lax.ppermute(array, "dp", [(i, 15 - i) for i in range(16)])


def dot(left, right, dims):
    return lax.dot_general(left, right, dims, preferred_element_type=F32)


def call(kernel, out_shape, arrays, flops, scalars=None, grid=(1,), in_specs=None, out_specs=None,
         scratch=(), name=None):
    whole = lambda s: pl.BlockSpec(s.shape, lambda *_, n=len(s.shape): (0,) * n)
    in_specs = in_specs or [whole(a) for a in arrays]
    outs = out_shape if isinstance(out_shape, (list, tuple)) else [out_shape]
    out_specs = out_specs or [whole(s) for s in outs]
    nbytes = sum(math.prod(a.shape) * a.dtype.itemsize for a in list(arrays) + list(outs))
    return pl.pallas_call(
        kernel,
        out_shape=list(outs),
        grid_spec=pltpu.PrefetchScalarGridSpec(
            num_scalar_prefetch=1, grid=grid, in_specs=in_specs, out_specs=out_specs,
            scratch_shapes=list(scratch),
        ),
        compiler_params=pltpu.CompilerParams(vmem_limit_bytes=VMEM_LIMIT),
        cost_estimate=pl.CostEstimate(flops=flops, bytes_accessed=nbytes, transcendentals=0),
        name=name,
    )(scalars, *arrays)


def block_of(j):
    return pl.BlockSpec((4 * TOK, UNIT), lambda i, s, j=j: (0, s[j]))


def whole_spec(a):
    return pl.BlockSpec(a.shape, lambda *_, n=len(a.shape): (0,) * n)


def project(rows, units, places, total):
    n = len(units)
    pieces = [p for u in units for p in u]

    def kernel(s_ref, *refs):
        row_refs, piece_refs, out_ref = refs[:n], list(refs[n : n + len(pieces)]), refs[-1]
        acc = refs[n + len(pieces)][...] if total is not None else None
        for j, u in enumerate(units):
            off = 0
            for p in u:
                size = p.shape[0]
                term = dot(row_refs[j][:, off : off + size], piece_refs.pop(0)[...], NN)
                acc = term if acc is None else acc + term
                off += size
        out_ref[...] = acc

    extra = [] if total is None else [total]
    return call(
        kernel, jax.ShapeDtypeStruct((4 * TOK, HALF_COLS), F32),
        [rows] * n + pieces + extra, 2 * 4 * TOK * UNIT * HALF_COLS * n, places,
        in_specs=[block_of(j) for j in range(n)] + [whole_spec(a) for a in pieces + extra],
        name="project",
    )[0]


def rotated(x, cosine, sine):
    return x * cosine + pltpu.roll(x, HD // 2, 1) * sine


def unrotated(y, cosine, sine):
    return y * cosine - pltpu.roll(y, HD // 2, 1) * sine


def inverse_rms(x):
    return lax.rsqrt(jnp.mean(x * x, -1, keepdims=True) + EPSILON)


def swap_halves(x):
    n = x.shape[0] // 2
    return jnp.concatenate([x[n:], x[:n]], 0)


def project_last(rows, unit, total, cosine, sine, gains, scalars):
    sizes = [p.shape[0] for p in unit]

    def kernel(s_ref, h_ref, *refs):
        pieces = refs[: len(sizes)]
        total_ref, cos_ref, sin_ref, gain_ref, q_ref, kv_ref, send_ref = refs[len(sizes) :]
        acc = total_ref[...]
        off = 0
        for size, p in zip(sizes, pieces):
            acc = acc + dot(h_ref[:, off : off + size], p[...], NN)
            off += size
        q_ref[...] = acc[:, :QCOLS]
        x = acc[:, QCOLS:]
        kv_ref[...] = x

        @pl.when(s_ref[1] == 0)
        def _():
            kn = x * inverse_rms(x) * gain_ref[1:2, :]
            send_ref[...] = rotated(kn, cos_ref[...], sin_ref[...]).astype(BF16)

        @pl.when(s_ref[1] != 0)
        def _():
            send_ref[...] = swap_halves(x.astype(BF16))

    arrays = [rows, *unit, total, cosine, sine, gains]
    shapes = [
        jax.ShapeDtypeStruct((4 * TOK, QCOLS), F32),
        jax.ShapeDtypeStruct((4 * TOK, HD), F32),
        jax.ShapeDtypeStruct((4 * TOK, HD), BF16),
    ]
    return call(
        kernel, shapes, arrays, 2 * 4 * TOK * UNIT * HALF_COLS, scalars,
        in_specs=[block_of(0)] + [whole_spec(a) for a in arrays[1:]], name="project_last",
    )


def attention(q, cotangent, kv_a, kv_b, rows, cosine, sine, gains, scalars):
    chips = 2
    chunk = chips * 2 * TOK
    lanes = HEADS * 2 * TOK
    queries = 2 * TOK

    def kernel(s_ref, q_ref, c_ref, a_ref, b_ref, rows_ref, cos_ref, sin_ref, gain_ref,
               gp_ref, gg_ref, mine_ref, other_ref, k_s, v_s, e_s, d_s):
        first = s_ref[1] == 0

        @pl.when(first)
        def _():
            k_s[...] = a_ref[...].reshape(SEQ, HD)
            v_s[...] = b_ref[...].reshape(SEQ, HD)

        @pl.when(jnp.logical_not(first))
        def _():
            k_s[...] = b_ref[...].reshape(SEQ, HD)
            v_s[...] = a_ref[...].reshape(SEQ, HD)

        cos = cos_ref[...].reshape(queries, HD)
        sin = sin_ref[...].reshape(queries, HD)
        gain = gain_ref[0:1, :]
        q_all = q_ref[...].reshape(queries, QCOLS)
        c_all = c_ref[...].reshape(queries, QCOLS)
        xs = [q_all[:, h * HD : (h + 1) * HD] for h in range(HEADS)]
        rms = [inverse_rms(x) for x in xs]
        qs = jnp.concatenate(
            [rotated(x * r * gain, cos, sin).astype(BF16) for x, r in zip(xs, rms)], 0
        )
        cs = jnp.concatenate([c_all[:, h * HD : (h + 1) * HD] for h in range(HEADS)], 0)
        half = lanes // 2
        start = rows_ref[0, 0:1, :half]
        place = rows_ref[0, 1:2, :half]
        total = jnp.zeros((1, lanes), F32)
        inner = jnp.zeros((1, lanes), F32)
        for c in range(SEQ // chunk):
            at = pl.ds(c * chunk, chunk)
            scores = dot(k_s[at, :], qs, NT)
            u = lax.broadcasted_iota(jnp.int32, (chunk, half), 0) + c * chunk
            seen = jnp.where((u >= start) & (u <= place), 1.0, 0.0)
            e = jnp.exp2(scores * EXP2_SCALE) * jnp.concatenate([seen, seen], 1)
            d = dot(v_s[at, :], cs, NT)
            total = total + jnp.sum(e, 0, keepdims=True)
            inner = inner + jnp.sum(e * d, 0, keepdims=True)
            e_s[at, :] = e
            d_s[at, :] = d
        inverse = 1.0 / total
        inner = inner * inverse
        grad_t = jnp.zeros((HD, lanes), F32)
        for c in range(SEQ // chunk):
            at = pl.ds(c * chunk, chunk)
            p = e_s[at, :] * inverse
            ds = (p * (d_s[at, :] - inner)).astype(BF16)
            dv = dot(p.astype(BF16), cs, NN).astype(BF16).reshape(chips, 2, 1, TOK, HD)
            dk = (dot(ds, qs, NN) * SCALING).astype(BF16).reshape(chips, 2, 1, TOK, HD)
            grad_t = grad_t + dot(k_s[at, :], ds, TN)
            own = pl.ds(c * chips, chips)

            @pl.when(first)
            def _():
                mine_ref[own] = dk
                other_ref[own] = dv

            @pl.when(jnp.logical_not(first))
            def _():
                mine_ref[own] = dv
                other_ref[own] = dk

        grad = grad_t.T * SCALING
        outs = []
        gain_sum = jnp.zeros((1, HD), F32)
        for h in range(HEADS):
            y = unrotated(grad[h * queries : (h + 1) * queries], cos, sin)
            x, r = xs[h], rms[h]
            weighted = y * gain
            mean = jnp.mean(x * weighted, -1, keepdims=True)
            outs.append((r * weighted - x * (r * r * r) * mean).astype(BF16))
            gain_sum = gain_sum + jnp.sum(y * (x * r), 0, keepdims=True)
        gp_ref[...] = jnp.concatenate(outs, 1).reshape(2, 1, TOK, QCOLS)
        gg_ref[...] = jnp.broadcast_to(gain_sum[None], (1, 8, HD))

    token_spec = lambda cols: pl.BlockSpec((2, 1, TOK, cols), lambda p, s: (0, p, 0, 0))
    kv_spec = pl.BlockSpec((CHIPS, 2, 1, TOK, HD), lambda p, s: (0, 0, p, 0, 0))
    shapes = [
        jax.ShapeDtypeStruct((2, 2, TOK, QCOLS), BF16),
        jax.ShapeDtypeStruct((2, 8, HD), F32),
        jax.ShapeDtypeStruct((CHIPS, 2, 2, TOK, HD), BF16),
        jax.ShapeDtypeStruct((CHIPS, 2, 2, TOK, HD), BF16),
    ]
    return call(
        kernel, shapes, [q, cotangent, kv_a, kv_b, rows, cosine, sine, gains],
        2 * 5 * 2 * SEQ * lanes * HD * 2, scalars, grid=(2,),
        in_specs=[
            token_spec(QCOLS), token_spec(QCOLS), kv_spec, kv_spec,
            pl.BlockSpec((1, 8, lanes), lambda p, s: (p, 0, 0)),
            token_spec(HD), token_spec(HD), whole_spec(gains),
        ],
        out_specs=[
            token_spec(QCOLS), pl.BlockSpec((1, 8, HD), lambda p, s: (p, 0, 0)), kv_spec, kv_spec,
        ],
        scratch=[
            pltpu.VMEM((SEQ, HD), BF16), pltpu.VMEM((SEQ, HD), BF16),
            pltpu.VMEM((SEQ, lanes), F32), pltpu.VMEM((SEQ, lanes), F32),
        ],
        name="attention",
    )


def kv_back(terms, kv, cosine, sine, gains, gain_parts, scalars):
    def kernel(s_ref, t_ref, kv_ref, cos_ref, sin_ref, gain_ref, gg_ref, out_ref):
        grad = t_ref[0].astype(F32)
        for i in range(1, CHIPS):
            grad = grad + t_ref[i].astype(F32)

        def put(values, key_sum):
            out_ref[: 4 * TOK, :] = values
            q_sum = gg_ref[0, 0:1, :] + gg_ref[1, 0:1, :]
            parts = []
            for s in (q_sum, key_sum):
                high = s.astype(BF16)
                rest = s - high.astype(F32)
                middle = rest.astype(BF16)
                parts += [high.astype(F32), middle.astype(F32), rest - middle.astype(F32)]
            parts.append(jnp.zeros((16 - len(parts), HD), F32))
            out_ref[4 * TOK :, :] = jnp.concatenate(parts, 0).astype(BF16)

        @pl.when(s_ref[1] == 0)
        def _():
            y = unrotated(grad, cos_ref[...], sin_ref[...])
            x = kv_ref[...]
            r = inverse_rms(x)
            weighted = y * gain_ref[1:2, :]
            mean = jnp.mean(x * weighted, -1, keepdims=True)
            values = (r * weighted - x * (r * r * r) * mean).astype(BF16)
            put(values, jnp.sum(y * (x * r), 0, keepdims=True))

        @pl.when(s_ref[1] != 0)
        def _():
            put(swap_halves(grad.astype(BF16)), jnp.zeros((1, HD), F32))

    return call(
        kernel, jax.ShapeDtypeStruct((4 * TOK + 16, HD), BF16),
        [terms, kv, cosine, sine, gains, gain_parts], 0, scalars, name="kv_back",
    )[0]


def hidden_grad(gp_q, gp_kv, pieces, scalars):
    def kernel(s_ref, q_ref, kv_ref, *refs):
        keep_ref, send_ref = refs[-2:]
        left = jnp.concatenate([q_ref[...], kv_ref[: 4 * TOK, :]], 1)
        for (place, off, piece), ref in zip(pieces, refs):
            size = piece.shape[0]
            col = pl.multiple_of(s_ref[place] * UNIT + off, 128)
            out = dot(left, ref[...], NT)
            for i in range(2):
                slot = s_ref[2] if i else 1 - s_ref[2]
                at = (pl.ds(pl.multiple_of(slot * TOK, TOK), TOK), pl.ds(col, size))
                keep_ref[at] = out[i * TOK : (i + 1) * TOK]
                send_ref[at] = out[(2 + i) * TOK : (3 + i) * TOK].astype(BF16)

    shapes = [
        jax.ShapeDtypeStruct((2 * TOK, CHIPS * UNIT), F32),
        jax.ShapeDtypeStruct((2 * TOK, CHIPS * UNIT), BF16),
    ]
    return call(
        kernel, shapes, [gp_q, gp_kv] + [p[2] for p in pieces],
        2 * 4 * TOK * CHIPS * UNIT * HALF_COLS, scalars, name="hidden_grad",
    )


def flat_gathered(parts):
    arrays, index = [], []
    for own, own_off, other, other_off in parts:
        for a in (own, other):
            if not any(a is b for b in arrays):
                arrays.append(a)
        find = lambda a: next(i for i, b in enumerate(arrays) if a is b)
        index.append((find(own), own_off, find(other), other_off))
    return arrays, index


def weight_grad_q(own, other, parts, scalars):
    arrays, index = flat_gathered(parts)

    def kernel(s_ref, own_ref, other_ref, *refs):
        mine_ref, send_ref, acc = refs[-3:]
        for j, (a, a_off, b, b_off) in enumerate(index):
            term = dot(own_ref[j], refs[a][a_off : a_off + 2 * TOK, :], TN)
            term = term + dot(other_ref[j], refs[b][b_off : b_off + 2 * TOK, :], TN)
            if j == 0:
                acc[...] = term
            else:
                acc[...] += term
        core = s_ref[1]
        rows = UNIT // 2
        mine_ref[...] = acc[pl.ds(pl.multiple_of(core * rows, rows), rows), :]
        send_ref[...] = acc[pl.ds(pl.multiple_of((1 - core) * rows, rows), rows), :]

    shape = jax.ShapeDtypeStruct((UNIT // 2, QCOLS), F32)
    return call(
        kernel, [shape, shape], [own, other] + arrays, 2 * SEQ * 2 * UNIT * QCOLS, scalars,
        scratch=[pltpu.VMEM((UNIT, QCOLS), F32)], name="weight_grad_q",
    )


def weight_grad_kv(own, other, parts, gain_rows, scalars):
    arrays, index = flat_gathered(parts)
    gain_at = [(next(i for i, b in enumerate(arrays) if a is b), off) for a, off in gain_rows]

    def kernel(s_ref, own_ref, other_ref, *refs):
        mine_ref, send_ref, gains_ref, acc = refs[-4:]
        total = None
        for j, (a, a_off, b, b_off) in enumerate(index):
            term = dot(refs[a][a_off : a_off + 2 * TOK, :], own_ref[j], TN)
            term = term + dot(refs[b][b_off : b_off + 2 * TOK, :], other_ref[j], TN)
            total = term if total is None else total + term
        acc[...] = total.T
        core = s_ref[1]
        rows = UNIT // 2
        mine_ref[...] = acc[pl.ds(pl.multiple_of(core * rows, rows), rows), :]
        send_ref[...] = acc[pl.ds(pl.multiple_of((1 - core) * rows, rows), rows), :]
        gains = None
        for a, off in gain_at:
            part = refs[a][off : off + 16, :].astype(F32)
            gains = part if gains is None else gains + part
        q_sum = gains[0:1] + gains[1:2] + gains[2:3]
        k_sum = gains[3:4] + gains[4:5] + gains[5:6]
        gains_ref[...] = jnp.concatenate([q_sum, k_sum, jnp.zeros((6, HD), F32)], 0)

    shape = jax.ShapeDtypeStruct((UNIT // 2, HD), F32)
    return call(
        kernel, [shape, shape, jax.ShapeDtypeStruct((8, HD), F32)], [own, other] + arrays,
        2 * SEQ * 2 * UNIT * HD, scalars, scratch=[pltpu.VMEM((UNIT, HD), F32)],
        name="weight_grad_kv",
    )


def gather_chips(unit):
    cut = 2 * TOK
    y1 = from_y(unit, 1)
    y3 = from_y(unit, 3)
    x0 = from_x(unit)
    y2a = from_y(y1[:cut], 1)
    y2b = from_y(y3[cut:], 3)
    x1 = from_y(x0, 1)
    x3 = from_y(x0, 3)
    x2a = from_y(x1[:cut], 1)
    x2b = from_y(x3[cut:], 3)
    parts = [(u, 0, u, cut) for u in (unit, y1, y3)] + [(y2a, 0, y2b, 0)]
    parts += [(u, 0, u, cut) for u in (x0, x1, x3)] + [(x2a, 0, x2b, 0)]
    return parts


def per_device(
    hidden, w_qkv, norm_gains, upstream, segment_ids, advantages, swap_slot, token_count
):
    data_rank = lax.axis_index("dp")
    shard = lax.axis_index("fsdp")
    core = shard % 2
    chip = shard // 2
    y = chip % 4
    x_hi = chip // 4
    first = core == 0
    slot = swap_slot[jnp.minimum(data_rank, 15 - data_rank)]

    def take(array, index):
        return lax.dynamic_index_in_dim(array, index, 0, keepdims=False)

    first_cols = jnp.concatenate([w_qkv[:, :512], w_qkv[:, 1024:1152]], 1)
    second_cols = jnp.concatenate([w_qkv[:, 512:1024], w_qkv[:, 1152:]], 1)
    mine = jnp.where(first, first_cols, second_cols)
    theirs = core_mate(jnp.where(first, second_cols, first_cols))
    unit = jnp.concatenate(
        [jnp.where(first, mine, theirs), jnp.where(first, theirs, mine)], 0
    )
    w_y1 = from_y(unit, 1)
    w_y3 = from_y(unit, 3)
    w_x0 = from_near_x(unit)
    w_y2a = from_y(w_y1[:384], 1)
    w_y2b = from_y(w_y3[384:], 3)
    w_x1a = from_y(w_x0[:256], 1)
    w_x1b = from_near_x(w_y1[256:])
    w_x3a = from_near_x(w_y3[:256])
    w_x3b = from_y(w_x0[256:], 3)
    w_x2a = from_y(w_x1a, 1)
    w_x2b = from_y(w_x3b, 3)
    place = lambda dx, dy: ((x_hi + dx) % 2) * 4 + (y + dy) % 4
    scalars = jnp.stack(
        [place(1, 2), core, slot, place(0, 0), place(0, 1), place(0, 3), place(0, 2),
         place(1, 0), place(1, 1), place(1, 3)]
    ).astype(jnp.int32)

    moved_small = jnp.concatenate(
        [take(segment_ids, slot).astype(BF16), take(advantages, slot), jnp.zeros((24,), BF16)]
    )
    moved_hidden = mirror(take(hidden, slot))
    moved_up = mirror(take(upstream, slot))
    moved_small = mirror(moved_small)
    kept_hidden = take(hidden, 1 - slot)
    segments = jnp.stack([take(segment_ids, 1 - slot), moved_small[:TOK].astype(jnp.int32)])
    advantage = jnp.stack([take(advantages, 1 - slot), moved_small[TOK : TOK + SEGS]])
    up = jnp.stack([take(upstream, 1 - slot), moved_up])
    own_rows = jnp.concatenate([kept_hidden, moved_hidden], 0)
    rows = jnp.concatenate(
        [own_rows, core_mate(kept_hidden), core_mate(moved_hidden)], 0
    )

    ids = jnp.arange(16, dtype=jnp.int32)
    below = jnp.sum((segments[:, :, None] < ids).astype(jnp.int32), 1)
    below = below + core_mate(below)
    for bit in (2, 4, 8):
        below = below + lax.ppermute(below, "fsdp", [(i, i ^ bit) for i in range(16)])
    segments_2 = jnp.stack([segments, core_mate(segments)])
    starts = jnp.sum(
        jnp.where(segments_2[..., None] == ids, below[None, :, None, :], 0), -1
    )
    local = jnp.arange(TOK, dtype=jnp.int32)
    slots = jnp.stack([shard * TOK + local, (shard ^ 1) * TOK + local])[:, None, :]
    slots = jnp.broadcast_to(slots, starts.shape)
    inverse = jnp.exp(-(jnp.arange(HD // 2, dtype=F32) * (2.0 / HD)) * THETA_LOG)
    angles = (slots - starts).astype(F32)[..., None] * inverse
    cosine = jnp.cos(angles)
    sine = jnp.sin(angles)
    cosine = jnp.concatenate([cosine, cosine], -1)
    sine = jnp.concatenate([-sine, sine], -1)
    cosine_flat = cosine.reshape(4 * TOK, HD)
    sine_flat = sine.reshape(4 * TOK, HD)

    def lane_rows(a):
        return jnp.tile(jnp.transpose(a, (1, 0, 2)).reshape(2, 2 * TOK), (1, HEADS))

    lanes = jnp.stack([lane_rows(starts), lane_rows(slots)], 1)
    lanes = jnp.concatenate([lanes, jnp.zeros((2, 6, lanes.shape[-1]), jnp.int32)], 1)

    table = (segments[..., None] == jnp.arange(SEGS, dtype=jnp.int32)).astype(F32)
    per_token = jnp.sum(table * advantage.astype(F32)[:, None, :], -1)
    factor = jnp.float32(2 * 16 * SEQ) / token_count[0].astype(F32)
    cotangent = (up.astype(F32) * (per_token * factor)[..., None]).astype(BF16)
    mine_cot = jnp.where(first, cotangent[..., :QCOLS], cotangent[..., QCOLS:])
    other_cot = core_mate(jnp.where(first, cotangent[..., QCOLS:], cotangent[..., :QCOLS]))
    cot = jnp.stack([mine_cot, other_cot])

    total = project(rows, [[unit], [w_y1], [w_y3], [w_x0]], scalars[jnp.array([3, 4, 5, 7])], None)
    total = project(
        rows, [[w_y2a, w_y2b], [w_x1a, w_x1b], [w_x3a, w_x3b]], scalars[jnp.array([6, 8, 9])], total
    )
    q, kv, send = project_last(
        rows, [w_x2a, w_x2b], total, cosine_flat, sine_flat, norm_gains, scalars
    )

    shape = (CHIPS, 4 * TOK, HD)
    gathered = lax.all_to_all(
        jnp.broadcast_to(send[None], shape), "fsdp", 0, 0, tiled=True,
        axis_index_groups=[list(range(0, 16, 2)), list(range(1, 16, 2))],
    )
    kv_shape = (CHIPS, 2, 2, TOK, HD)
    kv_other = core_mate(gathered).reshape(kv_shape)
    kv_mine = gathered.reshape(kv_shape)

    gp_q, gain_parts, grad_mine, grad_other = attention(
        q.reshape(2, 2, TOK, QCOLS), cot, kv_mine, kv_other, lanes, cosine, sine, norm_gains,
        scalars,
    )
    gp_q = gp_q.reshape(4 * TOK, QCOLS)

    near = lax.dynamic_slice_in_dim(own_rows, (1 - x_hi) * 4 * UNIT, 4 * UNIT, 1)
    near = from_x(near)
    blocks = {}
    for step in (0, 1, 3, 2):
        to = (y - step) % 4
        block = jnp.concatenate(
            [
                lax.dynamic_slice_in_dim(own_rows, (x_hi * 4 + to) * UNIT, UNIT, 1),
                lax.dynamic_slice_in_dim(near, to * UNIT, UNIT, 1),
            ],
            0,
        ).reshape(2, 2 * TOK, UNIT)
        blocks[step] = block if step == 0 else from_y(block, step)
    features = jnp.stack(
        [blocks[s][0] for s in (0, 1, 3, 2)] + [blocks[s][1] for s in (0, 1, 3, 2)]
    )
    features_other = core_mate(features)

    summed = (grad_mine.astype(F32) + core_mate(grad_other).astype(F32)).astype(BF16)
    terms = lax.all_to_all(
        summed.reshape(shape), "fsdp", 0, 0, tiled=True,
        axis_index_groups=[list(range(0, 16, 2)), list(range(1, 16, 2))],
    )
    parts_q = gather_chips(gp_q)
    gp_kv = kv_back(terms, kv, cosine_flat, sine_flat, norm_gains, gain_parts, scalars)
    parts_kv = gather_chips(gp_kv)

    keep, give = hidden_grad(
        gp_q, gp_kv,
        [(3, 0, unit), (4, 0, w_y1), (5, 0, w_y3), (6, 0, w_y2a), (6, 384, w_y2b), (7, 0, w_x0),
         (8, 0, w_x1a), (8, 256, w_x1b), (9, 0, w_x3a), (9, 256, w_x3b), (0, 0, w_x2a),
         (0, 256, w_x2b)],
        scalars,
    )
    grad_hidden = (keep + core_mate(give).astype(F32)).astype(BF16).reshape(hidden.shape)

    q_mine, q_give = weight_grad_q(features, features_other, parts_q, scalars)
    gain_rows = [(part[2], part[3] + 2 * TOK) for part in parts_kv]
    kv_mine, kv_give, gains = weight_grad_kv(
        features, features_other, parts_kv, gain_rows, scalars
    )
    q_got = core_mate(q_give)
    kv_got = core_mate(kv_give)
    grad_weight = jnp.concatenate(
        [
            jnp.where(first, q_mine, q_got), jnp.where(first, q_got, q_mine),
            jnp.where(first, kv_mine, kv_got), jnp.where(first, kv_got, kv_mine),
        ],
        1,
    )
    grad_gains = (gains + core_mate(gains))[:2]
    return (grad_hidden, grad_weight[None], grad_gains[None])


def solution(mesh):
    in_specs = (
        P("dp", "fsdp", None),
        P("fsdp", None),
        P(),
        P("dp", "fsdp", None),
        P("dp", "fsdp"),
        P("dp", None),
        P(),
        P(),
    )
    out_specs = (P("dp", "fsdp", None), P("dp", "fsdp", None), P("dp", None, None))
    return jax.shard_map(
        per_device, mesh=mesh, in_specs=in_specs, out_specs=out_specs, check_vma=False
    )
```

```python
import math

import jax
import jax.numpy as jnp
from jax import lax
from jax.experimental import pallas as pl
from jax.experimental.pallas import tpu as pltpu
from jax.sharding import PartitionSpec as P

HD = 128
HEADS = 4
TOK = 96
CHIPS = 8
UNIT = 640
HALF_COLS = 640
QCOLS = HEADS * HD
SEQ = 1536
SEGS = 8
EPSILON = 1e-06
THETA_LOG = math.log(1000000.0)
SCALING = 1.0 / math.sqrt(HD)
EXP2_SCALE = SCALING * math.log2(math.e)
F32 = jnp.float32
BF16 = jnp.bfloat16
NN = (((1,), (0,)), ((), ()))
NT = (((1,), (1,)), ((), ()))
TN = (((0,), (0,)), ((), ()))
VMEM_LIMIT = 56 * 1024 * 1024


def core_mate(array):
    return lax.ppermute(array, "fsdp", [(i, i ^ 1) for i in range(16)])


def from_y(array, step):
    def there(i):
        return (i & 8) | (((i // 2 - step) % 4) * 2) | (i & 1)

    return lax.ppermute(array, "fsdp", [(i, there(i)) for i in range(16)])


def from_x(array):
    return lax.ppermute(array, "fsdp", [(i, i ^ 8) for i in range(16)])


def from_near_x(array):
    pairs = [(d * 16 + i, (d ^ 8) * 16 + (i ^ 8)) for d in range(16) for i in range(16)]
    return lax.ppermute(array, ("dp", "fsdp"), pairs)


def mirror(array):
    return lax.ppermute(array, "dp", [(i, 15 - i) for i in range(16)])


def chips_exchange(blocks):
    return lax.all_to_all(
        blocks, "fsdp", 0, 0, tiled=True,
        axis_index_groups=[list(range(0, 16, 2)), list(range(1, 16, 2))],
    )


def after(array, *others):
    return lax.optimization_barrier((array, others))[0]


def dot(left, right, dims):
    return lax.dot_general(left, right, dims, preferred_element_type=F32)


def call(kernel, out_shape, arrays, flops, scalars=None, grid=(1,), in_specs=None, out_specs=None,
         scratch=(), name=None):
    whole = lambda s: pl.BlockSpec(s.shape, lambda *_, n=len(s.shape): (0,) * n)
    in_specs = in_specs or [whole(a) for a in arrays]
    outs = out_shape if isinstance(out_shape, (list, tuple)) else [out_shape]
    out_specs = out_specs or [whole(s) for s in outs]
    return pl.pallas_call(
        kernel,
        out_shape=list(outs),
        grid_spec=pltpu.PrefetchScalarGridSpec(
            num_scalar_prefetch=1, grid=grid, in_specs=in_specs, out_specs=out_specs,
            scratch_shapes=list(scratch),
        ),
        compiler_params=pltpu.CompilerParams(vmem_limit_bytes=VMEM_LIMIT),
        cost_estimate=pl.CostEstimate(flops=flops, bytes_accessed=0, transcendentals=0),
        name=name,
    )(scalars, *arrays)


def block_of(place):
    return pl.BlockSpec((2, TOK, UNIT), lambda i, s, j=place: (0, 0, s[j]))


def joined(own, other):
    return jnp.concatenate([own[0], other[0], own[1], other[1]], 0)


def whole_spec(a):
    return pl.BlockSpec(a.shape, lambda *_, n=len(a.shape): (0,) * n)


def project(rows, units, places, scalars, total):
    n = len(units)

    def kernel(s_ref, *refs):
        acc = refs[3 * n][...] if total is not None else None
        for j in range(n):
            term = dot(joined(refs[2 * j], refs[2 * j + 1]), refs[2 * n + j][...], NN)
            acc = term if acc is None else acc + term
        refs[-1][...] = acc

    extra = [] if total is None else [total]
    return call(
        kernel, jax.ShapeDtypeStruct((4 * TOK, HALF_COLS), F32),
        list(rows) * n + units + extra, 0, scalars,
        in_specs=[block_of(j) for j in places for _ in rows]
        + [whole_spec(a) for a in units + extra],
        name="project",
    )[0]


def rotated(x, cosine, sine):
    return x * cosine + pltpu.roll(x, HD // 2, 1) * sine


def unrotated(y, cosine, sine):
    return y * cosine - pltpu.roll(y, HD // 2, 1) * sine


def inverse_rms(x):
    return lax.rsqrt(jnp.mean(x * x, -1, keepdims=True) + EPSILON)


def swap_cores(x):
    return jnp.concatenate([x[i * TOK : (i + 1) * TOK] for i in (1, 0, 3, 2)], 0)


def project_last(rows, unit, total, cosine, sine, gains, scalars):
    def kernel(s_ref, own_ref, other_ref, low_ref, high_ref, total_ref, cos_ref, sin_ref,
               gain_ref, q_ref, kv_ref, send_ref):
        right = jnp.concatenate([low_ref[...], high_ref[...]], 0)
        acc = total_ref[...] + dot(joined(own_ref, other_ref), right, NN)
        q_ref[...] = acc[:, :QCOLS]
        x = acc[:, QCOLS:]
        kv_ref[...] = x

        @pl.when(s_ref[1] == 0)
        def _():
            kn = x * inverse_rms(x) * gain_ref[1:2, :]
            send_ref[...] = rotated(kn, cos_ref[...], sin_ref[...]).astype(BF16)

        @pl.when(s_ref[1] != 0)
        def _():
            send_ref[...] = swap_cores(x.astype(BF16))

    arrays = [*rows, *unit, total, cosine, sine, gains]
    shapes = [
        jax.ShapeDtypeStruct((4 * TOK, QCOLS), F32),
        jax.ShapeDtypeStruct((4 * TOK, HD), F32),
        jax.ShapeDtypeStruct((4 * TOK, HD), BF16),
    ]
    return call(
        kernel, shapes, arrays, 4 * 10**8, scalars,
        in_specs=[block_of(0)] * 2 + [whole_spec(a) for a in arrays[2:]], name="project_last",
    )


def positions(below, lanes, columns, scalars):
    def kernel(s_ref, below_ref, lanes_ref, cols_ref, cos_ref, sin_ref, out_ref):
        counts = jnp.sum(below_ref[...], 0)
        out_ref[...] = lanes_ref[...]
        seg = cols_ref[:, 0:1]
        pack = lax.broadcasted_iota(jnp.int32, (4 * TOK, 1), 0) // (2 * TOK)
        start = jnp.zeros((4 * TOK, 1), jnp.int32)
        for p in range(2):
            row = lanes_ref[p, 0:1, :]
            row_start = jnp.zeros(row.shape, jnp.int32)
            for k in range(1, SEGS + 1):
                count = counts[p : p + 1, k : k + 1]
                row_start = jnp.where(row == k, count, row_start)
                start = jnp.where((seg == k) & (pack == p), count, start)
            out_ref[p, 0:1, :] = row_start
        place = (cols_ref[:, 1:2] - start).astype(F32)
        lane = lax.broadcasted_iota(jnp.int32, (1, HD), 1)
        inverse = jnp.exp(-((lane % (HD // 2)).astype(F32) * (2.0 / HD)) * THETA_LOG)
        angles = place * inverse
        cos_ref[...] = jnp.cos(angles)
        sin_ref[...] = jnp.sin(angles) * jnp.where(lane < HD // 2, -1.0, 1.0)

    table = jax.ShapeDtypeStruct((4 * TOK, HD), F32)
    return call(
        kernel, [table, table, jax.ShapeDtypeStruct(lanes.shape, jnp.int32)],
        [below, lanes, columns], 0, scalars, name="positions",
    )


def attention(q, cotangent, kv_a, kv_b, rows, cosine, sine, gains, scalars, moved):
    chips = 2
    chunk = chips * 2 * TOK
    lanes = HEADS * 2 * TOK
    queries = 2 * TOK

    def kernel(s_ref, q_ref, c_ref, a_ref, b_ref, rows_ref, cos_ref, sin_ref, gain_ref,
               gp_ref, gg_ref, mine_ref, other_ref, k_s, v_s, e_s, d_s):
        first = s_ref[1] == 0

        @pl.when(first)
        def _():
            k_s[...] = a_ref[...].reshape(SEQ, HD)
            v_s[...] = b_ref[...].reshape(SEQ, HD)

        @pl.when(jnp.logical_not(first))
        def _():
            k_s[...] = b_ref[...].reshape(SEQ, HD)
            v_s[...] = a_ref[...].reshape(SEQ, HD)

        cos = cos_ref[...].reshape(queries, HD)
        sin = sin_ref[...].reshape(queries, HD)
        gain = gain_ref[0:1, :]
        q_all = q_ref[...].reshape(queries, QCOLS)
        c_all = c_ref[...].reshape(queries, QCOLS)
        xs = [q_all[:, h * HD : (h + 1) * HD] for h in range(HEADS)]
        rms = [inverse_rms(x) for x in xs]
        qs = jnp.concatenate(
            [rotated(x * r * gain, cos, sin).astype(BF16) for x, r in zip(xs, rms)], 0
        )
        cs = jnp.concatenate([c_all[:, h * HD : (h + 1) * HD] for h in range(HEADS)], 0)
        half = lanes // 2
        start = rows_ref[0, 0:1, :half]
        place = rows_ref[0, 1:2, :half]
        total = jnp.zeros((1, lanes), F32)
        inner = jnp.zeros((1, lanes), F32)
        for c in range(SEQ // chunk):
            at = pl.ds(c * chunk, chunk)
            scores = dot(k_s[at, :], qs, NT)
            u = lax.broadcasted_iota(jnp.int32, (chunk, half), 0) + c * chunk
            seen = jnp.where((u >= start) & (u <= place), 1.0, 0.0)
            e = jnp.exp2(scores * EXP2_SCALE) * jnp.concatenate([seen, seen], 1)
            d = dot(v_s[at, :], cs, NT)
            total = total + jnp.sum(e, 0, keepdims=True)
            inner = inner + jnp.sum(e * d, 0, keepdims=True)
            e_s[at, :] = e
            d_s[at, :] = d
        inverse = 1.0 / total
        inner = inner * inverse
        grad_t = jnp.zeros((HD, lanes), F32)
        for c in range(SEQ // chunk):
            at = pl.ds(c * chunk, chunk)
            p = e_s[at, :] * inverse
            ds = (p * (d_s[at, :] - inner)).astype(BF16)
            dv = dot(p.astype(BF16), cs, NN).astype(BF16).reshape(chips, 2, TOK, HD)
            dk = (dot(ds, qs, NN) * SCALING).astype(BF16).reshape(chips, 2, TOK, HD)
            grad_t = grad_t + dot(k_s[at, :], ds, TN)
            own = pl.ds(c * chips, chips)

            @pl.when(first)
            def _():
                mine_ref[own] = dk
                other_ref[own] = dv

            @pl.when(jnp.logical_not(first))
            def _():
                mine_ref[own] = dv
                other_ref[own] = dk

        grad = grad_t.T * SCALING
        outs = []
        gain_sum = jnp.zeros((1, HD), F32)
        for h in range(HEADS):
            y = unrotated(grad[h * queries : (h + 1) * queries], cos, sin)
            x, r = xs[h], rms[h]
            weighted = y * gain
            mean = jnp.mean(x * weighted, -1, keepdims=True)
            outs.append((r * weighted - x * (r * r * r) * mean).astype(BF16))
            gain_sum = gain_sum + jnp.sum(y * (x * r), 0, keepdims=True)
        gp_ref[...] = jnp.concatenate(outs, 1).reshape(2, TOK, QCOLS)
        gg_ref[...] = jnp.broadcast_to(gain_sum, (8, HD))

    pack = lambda s: s[2] if moved else 1 - s[2]
    token_spec = lambda cols: pl.BlockSpec((1, 2, TOK, cols), lambda i, s: (pack(s), 0, 0, 0))
    kv_spec = pl.BlockSpec((CHIPS, 1, 2, TOK, HD), lambda i, s: (0, pack(s), 0, 0, 0))
    shapes = [
        jax.ShapeDtypeStruct((2, TOK, QCOLS), BF16),
        jax.ShapeDtypeStruct((8, HD), F32),
        jax.ShapeDtypeStruct((CHIPS, 2, TOK, HD), BF16),
        jax.ShapeDtypeStruct((CHIPS, 2, TOK, HD), BF16),
    ]
    return call(
        kernel, shapes, [q, cotangent, kv_a, kv_b, rows, cosine, sine, gains],
        2 * 5 * 2 * SEQ * lanes * HD, scalars,
        in_specs=[
            token_spec(QCOLS), token_spec(QCOLS), kv_spec, kv_spec,
            pl.BlockSpec((1, 8, lanes), lambda i, s: (pack(s), 0, 0)),
            token_spec(HD), token_spec(HD), whole_spec(gains),
        ],
        scratch=[
            pltpu.VMEM((SEQ, HD), BF16), pltpu.VMEM((SEQ, HD), BF16),
            pltpu.VMEM((SEQ, lanes), F32), pltpu.VMEM((SEQ, lanes), F32),
        ],
        name="attention",
    )


def kv_back(terms, kv, cosine, sine, gains, gain_parts, scalars):
    rows = 2 * TOK

    def kernel(s_ref, t_ref, kv_ref, cos_ref, sin_ref, gain_ref, moved_ref, kept_ref, out_ref):
        grad = t_ref[0, 0].astype(F32)
        for i in range(1, CHIPS):
            grad = grad + t_ref[i, 0].astype(F32)
        q_sum = jnp.where(pl.program_id(0) == 0, moved_ref[0:1, :], kept_ref[0:1, :])

        def put(values, key_sum):
            parts = []
            for s in (q_sum, key_sum):
                high = s.astype(BF16)
                rest = s - high.astype(F32)
                middle = rest.astype(BF16)
                parts += [high.astype(F32), middle.astype(F32), rest - middle.astype(F32)]
            parts.append(jnp.zeros((16 - len(parts), HD), F32))
            out_ref[0, :rows, :] = values
            out_ref[0, rows:, :] = jnp.concatenate(parts, 0).astype(BF16)

        @pl.when(s_ref[1] == 0)
        def _():
            y = unrotated(grad, cos_ref[...], sin_ref[...])
            x = kv_ref[...]
            r = inverse_rms(x)
            weighted = y * gain_ref[1:2, :]
            mean = jnp.mean(x * weighted, -1, keepdims=True)
            values = (r * weighted - x * (r * r * r) * mean).astype(BF16)
            put(values, jnp.sum(y * (x * r), 0, keepdims=True))

        @pl.when(s_ref[1] != 0)
        def _():
            values = grad.astype(BF16)
            put(jnp.concatenate([values[TOK:], values[:TOK]], 0), jnp.zeros((1, HD), F32))

    pack_spec = pl.BlockSpec((rows, HD), lambda p, s: (s[2] + p - 2 * s[2] * p, 0))
    arrays = [terms, kv, cosine, sine, gains, *gain_parts]
    return call(
        kernel, jax.ShapeDtypeStruct((2, rows + 16, HD), BF16), arrays, 0, scalars, grid=(2,),
        in_specs=[pl.BlockSpec((CHIPS, 1, rows, HD), lambda p, s: (0, p, 0, 0))]
        + [pack_spec] * 3 + [whole_spec(a) for a in arrays[4:]],
        out_specs=[pl.BlockSpec((1, rows + 16, HD), lambda p, s: (p, 0, 0))],
        name="kv_back",
    )[0]


def hidden_grad(gp_q, gp_kv, units, scalars):
    def kernel(s_ref, q_ref, kv_ref, *refs):
        keep_ref, send_ref = refs[-2:]
        keys = jnp.concatenate([kv_ref[: 2 * TOK, :], kv_ref[2 * TOK + 16 : 4 * TOK + 16, :]], 0)
        left = jnp.concatenate([q_ref[...], keys], 1)
        refs = list(refs)
        for place, *pieces in units:
            col = pl.multiple_of(s_ref[place] * UNIT, 128)
            unit = jnp.concatenate([refs.pop(0)[...] for _ in pieces], 0)
            out = dot(left, unit, NT)
            for i in range(2):
                slot = s_ref[2] if i else 1 - s_ref[2]
                at = (pl.ds(pl.multiple_of(slot * TOK, TOK), TOK), pl.ds(col, UNIT))
                keep_ref[at] = out[2 * i * TOK : (2 * i + 1) * TOK]
                send_ref[at] = out[(2 * i + 1) * TOK : (2 * i + 2) * TOK].astype(BF16)

    shapes = [
        jax.ShapeDtypeStruct((2 * TOK, CHIPS * UNIT), F32),
        jax.ShapeDtypeStruct((2 * TOK, CHIPS * UNIT), BF16),
    ]
    return call(
        kernel, shapes, [gp_q, gp_kv] + [p for u in units for p in u[1:]],
        3 * 10**9, scalars, name="hidden_grad",
    )


def weight_grad(features, parts, cols, scalars, with_gains):
    arrays, index = [], []
    for part in parts:
        for a, at in part:
            if not any(a is b for b in arrays):
                arrays.append(a)
        index.append([(next(i for i, b in enumerate(arrays) if a is b), at) for a, at in part])

    def kernel(s_ref, *refs):
        places = (3, 4, 5, 6, 7, 8, 9, 0)
        feature_refs, refs = refs[:8], refs[8:]
        acc = refs[-1]
        total = None
        gains = None
        for j in range(0, CHIPS, 2):
            left, right = [], []
            for i in (j, j + 1):
                own, other = feature_refs[i % 4], feature_refs[4 + i % 4]
                left += [f[i // 4, pack] for pack in range(2) for f in (own, other)]
                rows = [refs[a][s_ref[places[i]] if at is None else at] for a, at in index[i]]
                if with_gains:
                    half = 2 * TOK + 16
                    part = rows[0][half - 16 : half].astype(F32)
                    part = part + rows[0][2 * half - 16 :].astype(F32)
                    gains = part if gains is None else gains + part
                    rows = [rows[0][: half - 16], rows[0][half : 2 * half - 16]]
                right += rows
            left, right = jnp.concatenate(left, 0), jnp.concatenate(right, 0)
            if with_gains:
                term = dot(right, left, TN)
                total = term if total is None else total + term
            elif j == 0:
                acc[...] = dot(left, right, TN)
            else:
                acc[...] += dot(left, right, TN)
        outs = refs[len(arrays) : -1]
        if with_gains:
            acc[...] = total.T
            q_sum = gains[0:1] + gains[1:2] + gains[2:3]
            k_sum = gains[3:4] + gains[4:5] + gains[5:6]
            outs[2][...] = jnp.concatenate([q_sum, k_sum, jnp.zeros((6, HD), F32)], 0)
        core = s_ref[1]
        rows = UNIT // 2
        outs[0][...] = acc[pl.ds(pl.multiple_of(core * rows, rows), rows), :]
        outs[1][...] = acc[pl.ds(pl.multiple_of((1 - core) * rows, rows), rows), :]

    shape = jax.ShapeDtypeStruct((UNIT // 2, cols), F32)
    shapes = [shape, shape]
    if with_gains:
        shapes.append(jax.ShapeDtypeStruct((8, HD), F32))
    return call(
        kernel, shapes, [*features] + arrays, 4 * 10**10 if with_gains else 3 * 10**9, scalars,
        scratch=[pltpu.VMEM((UNIT, cols), F32)],
        name="weight_grad_kv" if with_gains else "weight_grad_q",
    )


def gather_near(unit):
    return from_y(unit, 1), from_y(unit, 3), from_x(unit)


def gather_far(unit, near):
    y1, y3, x0 = near
    y2 = from_y(y1, 1)
    x1 = from_y(x0, 1)
    x3 = from_y(x0, 3)
    cut = 2 * TOK
    x2 = [from_y(x1[:cut], 1), from_y(x3[cut:], 3)]
    parts = [[(u, slice(None))] for u in (unit, y1, y3, y2, x0, x1, x3)]
    return parts + [[(u, slice(None)) for u in x2]]


def per_device(
    hidden, w_qkv, norm_gains, upstream, segment_ids, advantages, swap_slot, token_count
):
    data_rank = lax.axis_index("dp")
    shard = lax.axis_index("fsdp")
    core = shard % 2
    chip = shard // 2
    y = chip % 4
    x_hi = chip // 4
    first = core == 0
    slot = swap_slot[jnp.minimum(data_rank, 15 - data_rank)]

    def take(array, index):
        return lax.dynamic_index_in_dim(array, index, 0, keepdims=False)

    first_cols = jnp.concatenate([w_qkv[:, :512], w_qkv[:, 1024:1152]], 1)
    second_cols = jnp.concatenate([w_qkv[:, 512:1024], w_qkv[:, 1152:]], 1)
    mine = jnp.where(first, first_cols, second_cols)
    theirs = core_mate(jnp.where(first, second_cols, first_cols))
    low = jnp.where(first, mine, theirs)
    high = jnp.where(first, theirs, mine)
    unit = jnp.concatenate([low, high], 0)

    place = lambda dx, dy: ((x_hi + dx) % 2) * 4 + (y + dy) % 4
    scalars = jnp.stack(
        [place(1, 2), core, slot, place(0, 0), place(0, 1), place(0, 3), place(0, 2),
         place(1, 0), place(1, 1), place(1, 3)]
    ).astype(jnp.int32)

    ids = jnp.arange(16, dtype=jnp.int32)
    below = jnp.sum((segment_ids[:, :, None] < ids).astype(jnp.int32), 1)
    below = lax.all_to_all(
        jnp.broadcast_to(below[None], (16, 2, 16)), "fsdp", 0, 0, tiled=True
    )
    segments = jnp.stack([segment_ids, core_mate(segment_ids)], 1)
    local = jnp.arange(TOK, dtype=jnp.int32)
    slots = jnp.stack([shard * TOK + local, (shard ^ 1) * TOK + local])[None]
    slots = jnp.broadcast_to(slots, segments.shape)

    def lane_rows(a):
        return jnp.tile(a.reshape(2, 2 * TOK), (1, HEADS))

    lanes = jnp.stack([lane_rows(segments), lane_rows(slots)], 1)
    lanes = jnp.concatenate([lanes, jnp.zeros((2, 6, lanes.shape[-1]), jnp.int32)], 1)
    columns = jnp.concatenate(
        [segments.reshape(4 * TOK, 1), slots.reshape(4 * TOK, 1)], 1
    )

    table = (segment_ids[..., None] == jnp.arange(SEGS, dtype=jnp.int32)).astype(F32)
    per_token = jnp.sum(table * advantages.astype(F32)[:, None, :], -1)
    factor = jnp.float32(2 * 16 * SEQ) / token_count[0].astype(F32)
    cotangent = (upstream.astype(F32) * (per_token * factor)[..., None]).astype(BF16)
    mine_cot = jnp.where(first, cotangent[..., :QCOLS], cotangent[..., QCOLS:])
    other_cot = core_mate(jnp.where(first, cotangent[..., QCOLS:], cotangent[..., :QCOLS]))
    cot = jnp.stack([mine_cot, other_cot], 1)

    rows = [hidden, core_mate(hidden)]
    unit, below, lanes, columns = lax.optimization_barrier((unit, below, lanes, columns))
    y1, y3, x0 = from_y(unit, 1), from_y(unit, 3), from_near_x(unit)
    tables = positions(below, lanes, columns, scalars)
    y1, y3, x0, tables, cot = lax.optimization_barrier((y1, y3, x0, tables, cot))
    cosine_flat, sine_flat, lanes = tables
    cosine = cosine_flat.reshape(2, 2, TOK, HD)
    sine = sine_flat.reshape(2, 2, TOK, HD)
    y2, x1, x3 = from_y(y1, 1), from_near_x(y1), from_y(x0, 3)
    y2, x1, x3 = lax.optimization_barrier((y2, x1, x3))
    x2_a, x2_b = from_y(x1[: UNIT // 2], 1), from_y(x3[UNIT // 2 :], 3)
    total = project(rows, [unit, y1, y3, x0], [3, 4, 5, 7], scalars, None)
    total = project(rows, [y2, x1, x3], [6, 8, 9], scalars, total)
    x2_a, x2_b, total = lax.optimization_barrier((x2_a, x2_b, total))
    q, kv, send = project_last(
        rows, [x2_a, x2_b], total, cosine_flat, sine_flat, norm_gains, scalars
    )

    moved = mirror(take(hidden, slot))
    own_rows = jnp.stack([take(hidden, 1 - slot), moved])
    near = from_x(lax.dynamic_slice_in_dim(own_rows, (1 - x_hi) * 4 * UNIT, 4 * UNIT, 2))
    blocks = []
    for step in (0, 1, 3, 2):
        to = (y - step) % 4
        blocks.append(
            jnp.stack(
                [
                    lax.dynamic_slice_in_dim(own_rows, (x_hi * 4 + to) * UNIT, UNIT, 2),
                    lax.dynamic_slice_in_dim(near, to * UNIT, UNIT, 2),
                ]
            )
        )

    shape = (CHIPS, 4 * TOK, HD)
    gathered = chips_exchange(jnp.broadcast_to(send[None], shape))
    gathered, blocks = lax.optimization_barrier((gathered, blocks))
    blocks = [blocks[0], from_y(blocks[1], 1), from_y(blocks[2], 3), from_y(blocks[3], 2)]
    kv_shape = (CHIPS, 2, 2, TOK, HD)
    kv_other = core_mate(gathered).reshape(kv_shape)
    kv_mine = gathered.reshape(kv_shape)

    def attend(moved):
        return attention(
            q.reshape(2, 2, TOK, QCOLS), cot, kv_mine, kv_other, lanes, cosine, sine, norm_gains,
            scalars, moved,
        )

    gp_moved, gain_moved, moved_mine, moved_other = attend(True)
    gp_kept, gain_kept, kept_mine, kept_other = attend(False)
    kept_other, blocks = lax.optimization_barrier((kept_other, blocks))
    gp_q = jnp.concatenate([gp_kept, mirror(gp_moved)], 0).reshape(4 * TOK, QCOLS)

    summed = jnp.stack(
        [
            moved_mine.astype(F32) + core_mate(moved_other).astype(F32),
            kept_mine.astype(F32) + core_mate(kept_other).astype(F32),
        ],
        1,
    ).astype(BF16)
    terms = chips_exchange(summed.reshape(CHIPS, 2, 2 * TOK, HD))
    near_q = gather_near(gp_q)
    terms = after(terms, *near_q)
    parts_q = gather_far(gp_q, near_q)
    gp_kv = kv_back(
        terms, kv, cosine_flat, sine_flat, norm_gains, (gain_moved, gain_kept), scalars
    )
    gp_kv = jnp.concatenate([gp_kv[1], mirror(gp_kv[0])], 0)
    gp_kv = after(gp_kv, [part[0][0] for part in parts_q])
    parts_kv = chips_exchange(jnp.broadcast_to(gp_kv[None], (CHIPS, 4 * TOK + 32, HD)))

    pieces = [
        (3, unit), (4, y1), (5, y3), (6, y2), (7, x0), (8, x1), (9, x3), (0, x2_a, x2_b),
    ]
    keep, give = hidden_grad(gp_q, gp_kv, pieces, scalars)
    grad_hidden = (keep + core_mate(give).astype(F32)).astype(BF16).reshape(hidden.shape)

    features = blocks + [core_mate(b) for b in blocks]
    q_mine, q_give = weight_grad(features, parts_q, QCOLS, scalars, False)
    kv_mine, kv_give, gains = weight_grad(
        features, [[(parts_kv, None)]] * CHIPS, HD, scalars, True
    )
    q_got = core_mate(q_give)
    kv_got = core_mate(kv_give)
    grad_weight = jnp.concatenate(
        [
            jnp.where(first, q_mine, q_got), jnp.where(first, q_got, q_mine),
            jnp.where(first, kv_mine, kv_got), jnp.where(first, kv_got, kv_mine),
        ],
        1,
    )
    grad_gains = (gains + core_mate(gains))[:2]
    return (grad_hidden, grad_weight[None], grad_gains[None])


def solution(mesh):
    in_specs = (
        P("dp", "fsdp", None),
        P("fsdp", None),
        P(),
        P("dp", "fsdp", None),
        P("dp", "fsdp"),
        P("dp", None),
        P(),
        P(),
    )
    out_specs = (P("dp", "fsdp", None), P("dp", "fsdp", None), P("dp", None, None))
    return jax.shard_map(
        per_device, mesh=mesh, in_specs=in_specs, out_specs=out_specs, check_vma=False
    )
```

```python
import math

import jax
import jax.numpy as jnp
from jax import lax
from jax.experimental import pallas as pl
from jax.experimental.pallas import tpu as pltpu
from jax.sharding import PartitionSpec as P

HD = 128
HEADS = 4
TOK = 96
CHIPS = 8
UNIT = 640
HALF_COLS = 640
QCOLS = HEADS * HD
SEQ = 1536
SEGS = 8
EPSILON = 1e-06
THETA_LOG = math.log(1000000.0)
SCALING = 1.0 / math.sqrt(HD)
EXP2_SCALE = SCALING * math.log2(math.e)
F32 = jnp.float32
BF16 = jnp.bfloat16
NN = (((1,), (0,)), ((), ()))
NT = (((1,), (1,)), ((), ()))
TN = (((0,), (0,)), ((), ()))
VMEM_LIMIT = 56 * 1024 * 1024


def core_mate(array):
    return lax.ppermute(array, "fsdp", [(i, i ^ 1) for i in range(16)])


def from_y(array, step):
    def there(i):
        return (i & 8) | (((i // 2 - step) % 4) * 2) | (i & 1)

    return lax.ppermute(array, "fsdp", [(i, there(i)) for i in range(16)])


def from_x(array):
    return lax.ppermute(array, "fsdp", [(i, i ^ 8) for i in range(16)])


def from_near_x(array):
    pairs = [(d * 16 + i, (d ^ 8) * 16 + (i ^ 8)) for d in range(16) for i in range(16)]
    return lax.ppermute(array, ("dp", "fsdp"), pairs)


def mirror(array):
    return lax.ppermute(array, "dp", [(i, 15 - i) for i in range(16)])


def chips_exchange(blocks):
    return lax.all_to_all(
        blocks, "fsdp", 0, 0, tiled=True,
        axis_index_groups=[list(range(0, 16, 2)), list(range(1, 16, 2))],
    )


def after(array, *others):
    return lax.optimization_barrier((array, others))[0]


def dot(left, right, dims):
    return lax.dot_general(left, right, dims, preferred_element_type=F32)


def call(kernel, out_shape, arrays, flops, scalars=None, grid=(1,), in_specs=None, out_specs=None,
         scratch=(), name=None):
    whole = lambda s: pl.BlockSpec(s.shape, lambda *_, n=len(s.shape): (0,) * n)
    in_specs = in_specs or [whole(a) for a in arrays]
    outs = out_shape if isinstance(out_shape, (list, tuple)) else [out_shape]
    out_specs = out_specs or [whole(s) for s in outs]
    return pl.pallas_call(
        kernel,
        out_shape=list(outs),
        grid_spec=pltpu.PrefetchScalarGridSpec(
            num_scalar_prefetch=1, grid=grid, in_specs=in_specs, out_specs=out_specs,
            scratch_shapes=list(scratch),
        ),
        compiler_params=pltpu.CompilerParams(vmem_limit_bytes=VMEM_LIMIT),
        cost_estimate=pl.CostEstimate(flops=flops, bytes_accessed=0, transcendentals=0),
        name=name,
    )(scalars, *arrays)


def block_of(place):
    return pl.BlockSpec((2, TOK, UNIT), lambda i, s, j=place: (0, 0, s[j]))


def joined(own, other):
    return jnp.concatenate([own[0], other[0], own[1], other[1]], 0)


def whole_spec(a):
    return pl.BlockSpec(a.shape, lambda *_, n=len(a.shape): (0,) * n)


def project(rows, units, places, scalars, total):
    n = len(units)

    def kernel(s_ref, *refs):
        acc = refs[3 * n][...] if total is not None else None
        for j in range(n):
            term = dot(joined(refs[2 * j], refs[2 * j + 1]), refs[2 * n + j][...], NN)
            acc = term if acc is None else acc + term
        refs[-1][...] = acc

    extra = [] if total is None else [total]
    return call(
        kernel, jax.ShapeDtypeStruct((4 * TOK, HALF_COLS), F32),
        list(rows) * n + units + extra, 0, scalars,
        in_specs=[block_of(j) for j in places for _ in rows]
        + [whole_spec(a) for a in units + extra],
        name="project",
    )[0]


def rotated(x, cosine, sine):
    return x * cosine + pltpu.roll(x, HD // 2, 1) * sine


def unrotated(y, cosine, sine):
    return y * cosine - pltpu.roll(y, HD // 2, 1) * sine


def inverse_rms(x):
    return lax.rsqrt(jnp.mean(x * x, -1, keepdims=True) + EPSILON)


def swap_cores(x):
    return jnp.concatenate([x[i * TOK : (i + 1) * TOK] for i in (1, 0, 3, 2)], 0)


def project_last(rows, unit, total, cosine, sine, gains, scalars):
    def kernel(s_ref, own_ref, other_ref, low_ref, high_ref, total_ref, cos_ref, sin_ref,
               gain_ref, q_ref, kv_ref, send_ref):
        right = jnp.concatenate([low_ref[...], high_ref[...]], 0)
        acc = total_ref[...] + dot(joined(own_ref, other_ref), right, NN)
        q_ref[...] = acc[:, :QCOLS]
        x = acc[:, QCOLS:]
        kv_ref[...] = x

        @pl.when(s_ref[1] == 0)
        def _():
            kn = x * inverse_rms(x) * gain_ref[1:2, :]
            kr = rotated(kn, cos_ref[...], sin_ref[...]).astype(BF16)
            for i in range(CHIPS):
                send_ref[i] = kr

        @pl.when(s_ref[1] != 0)
        def _():
            v = swap_cores(x.astype(BF16))
            for i in range(CHIPS):
                send_ref[i] = v

    arrays = [*rows, *unit, total, cosine, sine, gains]
    shapes = [
        jax.ShapeDtypeStruct((4 * TOK, QCOLS), F32),
        jax.ShapeDtypeStruct((4 * TOK, HD), F32),
        jax.ShapeDtypeStruct((CHIPS, 4 * TOK, HD), BF16),
    ]
    return call(
        kernel, shapes, arrays, 4 * 10**8, scalars,
        in_specs=[block_of(0)] * 2 + [whole_spec(a) for a in arrays[2:]], name="project_last",
    )


def positions(below, lanes, columns, scalars):
    def kernel(s_ref, below_ref, lanes_ref, cols_ref, cos_ref, sin_ref, out_ref):
        counts = jnp.sum(below_ref[...], 0)
        out_ref[...] = lanes_ref[...]
        seg = cols_ref[:, 0:1]
        pack = lax.broadcasted_iota(jnp.int32, (4 * TOK, 1), 0) // (2 * TOK)
        start = jnp.zeros((4 * TOK, 1), jnp.int32)
        for p in range(2):
            row = lanes_ref[p, 0:1, :]
            row_start = jnp.zeros(row.shape, jnp.int32)
            for k in range(1, SEGS + 1):
                count = counts[p : p + 1, k : k + 1]
                row_start = jnp.where(row == k, count, row_start)
                start = jnp.where((seg == k) & (pack == p), count, start)
            out_ref[p, 0:1, :] = row_start
        place = (cols_ref[:, 1:2] - start).astype(F32)
        lane = lax.broadcasted_iota(jnp.int32, (1, HD), 1)
        inverse = jnp.exp(-((lane % (HD // 2)).astype(F32) * (2.0 / HD)) * THETA_LOG)
        angles = place * inverse
        cos_ref[...] = jnp.cos(angles)
        sin_ref[...] = jnp.sin(angles) * jnp.where(lane < HD // 2, -1.0, 1.0)

    table = jax.ShapeDtypeStruct((4 * TOK, HD), F32)
    return call(
        kernel, [table, table, jax.ShapeDtypeStruct(lanes.shape, jnp.int32)],
        [below, lanes, columns], 0, scalars, name="positions",
    )


def attention(q, cotangent, kv_a, kv_b, rows, cosine, sine, gains, scalars, moved):
    chips = 2
    chunk = chips * 2 * TOK
    lanes = HEADS * 2 * TOK
    queries = 2 * TOK

    def kernel(s_ref, q_ref, c_ref, a_ref, b_ref, rows_ref, cos_ref, sin_ref, gain_ref,
               gp_ref, gg_ref, mine_ref, other_ref, k_s, v_s, e_s, d_s):
        first = s_ref[1] == 0

        @pl.when(first)
        def _():
            k_s[...] = a_ref[...].reshape(SEQ, HD)
            v_s[...] = b_ref[...].reshape(SEQ, HD)

        @pl.when(jnp.logical_not(first))
        def _():
            k_s[...] = b_ref[...].reshape(SEQ, HD)
            v_s[...] = a_ref[...].reshape(SEQ, HD)

        cos = cos_ref[...].reshape(queries, HD)
        sin = sin_ref[...].reshape(queries, HD)
        gain = gain_ref[0:1, :]
        q_all = q_ref[...].reshape(queries, QCOLS)
        c_all = c_ref[...].reshape(queries, QCOLS)
        xs = [q_all[:, h * HD : (h + 1) * HD] for h in range(HEADS)]
        rms = [inverse_rms(x) for x in xs]
        qs = jnp.concatenate(
            [rotated(x * r * gain, cos, sin).astype(BF16) for x, r in zip(xs, rms)], 0
        )
        cs = jnp.concatenate([c_all[:, h * HD : (h + 1) * HD] for h in range(HEADS)], 0)
        half = lanes // 2
        start = rows_ref[0, 0:1, :half]
        place = rows_ref[0, 1:2, :half]
        total = jnp.zeros((1, lanes), F32)
        inner = jnp.zeros((1, lanes), F32)
        for c in range(SEQ // chunk):
            at = pl.ds(c * chunk, chunk)
            scores = dot(k_s[at, :], qs, NT)
            u = lax.broadcasted_iota(jnp.int32, (chunk, half), 0) + c * chunk
            seen = jnp.where((u >= start) & (u <= place), 1.0, 0.0)
            e = jnp.exp2(scores * EXP2_SCALE) * jnp.concatenate([seen, seen], 1)
            d = dot(v_s[at, :], cs, NT)
            total = total + jnp.sum(e, 0, keepdims=True)
            inner = inner + jnp.sum(e * d, 0, keepdims=True)
            e_s[at, :] = e
            d_s[at, :] = d
        inverse = 1.0 / total
        inner = inner * inverse
        grad_t = jnp.zeros((HD, lanes), F32)
        for c in range(SEQ // chunk):
            at = pl.ds(c * chunk, chunk)
            p = e_s[at, :] * inverse
            ds = (p * (d_s[at, :] - inner)).astype(BF16)
            dv = dot(p.astype(BF16), cs, NN).astype(BF16).reshape(chips, 2, TOK, HD)
            dk = (dot(ds, qs, NN) * SCALING).astype(BF16).reshape(chips, 2, TOK, HD)
            grad_t = grad_t + dot(k_s[at, :], ds, TN)
            own = pl.ds(c * chips, chips)

            @pl.when(first)
            def _():
                mine_ref[own] = dk
                other_ref[own] = dv

            @pl.when(jnp.logical_not(first))
            def _():
                mine_ref[own] = dv
                other_ref[own] = dk

        grad = grad_t.T * SCALING
        outs = []
        gain_sum = jnp.zeros((1, HD), F32)
        for h in range(HEADS):
            y = unrotated(grad[h * queries : (h + 1) * queries], cos, sin)
            x, r = xs[h], rms[h]
            weighted = y * gain
            mean = jnp.mean(x * weighted, -1, keepdims=True)
            outs.append((r * weighted - x * (r * r * r) * mean).astype(BF16))
            gain_sum = gain_sum + jnp.sum(y * (x * r), 0, keepdims=True)
        gp_ref[...] = jnp.concatenate(outs, 1).reshape(2, TOK, QCOLS)
        gg_ref[...] = jnp.broadcast_to(gain_sum, (8, HD))

    pack = lambda s: s[2] if moved else 1 - s[2]
    token_spec = lambda cols: pl.BlockSpec((1, 2, TOK, cols), lambda i, s: (pack(s), 0, 0, 0))
    kv_spec = pl.BlockSpec((CHIPS, 1, 2, TOK, HD), lambda i, s: (0, pack(s), 0, 0, 0))
    shapes = [
        jax.ShapeDtypeStruct((2, TOK, QCOLS), BF16),
        jax.ShapeDtypeStruct((8, HD), F32),
        jax.ShapeDtypeStruct((CHIPS, 2, TOK, HD), BF16),
        jax.ShapeDtypeStruct((CHIPS, 2, TOK, HD), BF16),
    ]
    return call(
        kernel, shapes, [q, cotangent, kv_a, kv_b, rows, cosine, sine, gains],
        2 * 5 * 2 * SEQ * lanes * HD, scalars,
        in_specs=[
            token_spec(QCOLS), token_spec(QCOLS), kv_spec, kv_spec,
            pl.BlockSpec((1, 8, lanes), lambda i, s: (pack(s), 0, 0)),
            token_spec(HD), token_spec(HD), whole_spec(gains),
        ],
        scratch=[
            pltpu.VMEM((SEQ, HD), BF16), pltpu.VMEM((SEQ, HD), BF16),
            pltpu.VMEM((SEQ, lanes), F32), pltpu.VMEM((SEQ, lanes), F32),
        ],
        name="attention",
    )


def kv_back(terms, kv, cosine, sine, gains, gain_parts, scalars):
    rows = 2 * TOK

    def kernel(s_ref, t_ref, kv_ref, cos_ref, sin_ref, gain_ref, moved_ref, kept_ref, out_ref):
        grad = t_ref[0, 0].astype(F32)
        for i in range(1, CHIPS):
            grad = grad + t_ref[i, 0].astype(F32)
        q_sum = jnp.where(pl.program_id(0) == 0, moved_ref[0:1, :], kept_ref[0:1, :])

        def put(values, key_sum):
            parts = []
            for s in (q_sum, key_sum):
                high = s.astype(BF16)
                rest = s - high.astype(F32)
                middle = rest.astype(BF16)
                parts += [high.astype(F32), middle.astype(F32), rest - middle.astype(F32)]
            parts.append(jnp.zeros((16 - len(parts), HD), F32))
            out_ref[0, :rows, :] = values
            out_ref[0, rows:, :] = jnp.concatenate(parts, 0).astype(BF16)

        @pl.when(s_ref[1] == 0)
        def _():
            y = unrotated(grad, cos_ref[...], sin_ref[...])
            x = kv_ref[...]
            r = inverse_rms(x)
            weighted = y * gain_ref[1:2, :]
            mean = jnp.mean(x * weighted, -1, keepdims=True)
            values = (r * weighted - x * (r * r * r) * mean).astype(BF16)
            put(values, jnp.sum(y * (x * r), 0, keepdims=True))

        @pl.when(s_ref[1] != 0)
        def _():
            values = grad.astype(BF16)
            put(jnp.concatenate([values[TOK:], values[:TOK]], 0), jnp.zeros((1, HD), F32))

    pack_spec = pl.BlockSpec((rows, HD), lambda p, s: (s[2] + p - 2 * s[2] * p, 0))
    arrays = [terms, kv, cosine, sine, gains, *gain_parts]
    return call(
        kernel, jax.ShapeDtypeStruct((2, rows + 16, HD), BF16), arrays, 0, scalars, grid=(2,),
        in_specs=[pl.BlockSpec((CHIPS, 1, rows, HD), lambda p, s: (0, p, 0, 0))]
        + [pack_spec] * 3 + [whole_spec(a) for a in arrays[4:]],
        out_specs=[pl.BlockSpec((1, rows + 16, HD), lambda p, s: (p, 0, 0))],
        name="kv_back",
    )[0]


def hidden_grad(gp_q, gp_kv, units, scalars):
    def kernel(s_ref, q_ref, kv_ref, *refs):
        keep_ref, send_ref = refs[-2:]
        keys = jnp.concatenate([kv_ref[: 2 * TOK, :], kv_ref[2 * TOK + 16 : 4 * TOK + 16, :]], 0)
        left = jnp.concatenate([q_ref[...], keys], 1)
        refs = list(refs)
        for place, *pieces in units:
            col = pl.multiple_of(s_ref[place] * UNIT, 128)
            unit = jnp.concatenate([refs.pop(0)[...] for _ in pieces], 0)
            out = dot(left, unit, NT)
            for i in range(2):
                slot = s_ref[2] if i else 1 - s_ref[2]
                at = (pl.ds(pl.multiple_of(slot * TOK, TOK), TOK), pl.ds(col, UNIT))
                keep_ref[at] = out[2 * i * TOK : (2 * i + 1) * TOK]
                send_ref[at] = out[(2 * i + 1) * TOK : (2 * i + 2) * TOK].astype(BF16)

    shapes = [
        jax.ShapeDtypeStruct((2 * TOK, CHIPS * UNIT), F32),
        jax.ShapeDtypeStruct((2 * TOK, CHIPS * UNIT), BF16),
    ]
    return call(
        kernel, shapes, [gp_q, gp_kv] + [p for u in units for p in u[1:]],
        3 * 10**9, scalars, name="hidden_grad",
    )


def weight_grad(features, parts, cols, scalars, with_gains):
    arrays, index = [], []
    for part in parts:
        for a, at in part:
            if not any(a is b for b in arrays):
                arrays.append(a)
        index.append([(next(i for i, b in enumerate(arrays) if a is b), at) for a, at in part])

    def kernel(s_ref, *refs):
        places = (3, 4, 5, 6, 7, 8, 9, 0)
        feature_refs, refs = refs[:8], refs[8:]
        acc = refs[-1]
        total = None
        gains = None
        for j in range(0, CHIPS, 2):
            left, right = [], []
            for i in (j, j + 1):
                own, other = feature_refs[i % 4], feature_refs[4 + i % 4]
                left += [f[i // 4, pack] for pack in range(2) for f in (own, other)]
                rows = [refs[a][s_ref[places[i]] if at is None else at] for a, at in index[i]]
                if with_gains:
                    half = 2 * TOK + 16
                    part = rows[0][half - 16 : half].astype(F32)
                    part = part + rows[0][2 * half - 16 :].astype(F32)
                    gains = part if gains is None else gains + part
                    rows = [rows[0][: half - 16], rows[0][half : 2 * half - 16]]
                right += rows
            left, right = jnp.concatenate(left, 0), jnp.concatenate(right, 0)
            if with_gains:
                term = dot(right, left, TN)
                total = term if total is None else total + term
            elif j == 0:
                acc[...] = dot(left, right, TN)
            else:
                acc[...] += dot(left, right, TN)
        outs = refs[len(arrays) : -1]
        if with_gains:
            acc[...] = total.T
            q_sum = gains[0:1] + gains[1:2] + gains[2:3]
            k_sum = gains[3:4] + gains[4:5] + gains[5:6]
            outs[2][...] = jnp.concatenate([q_sum, k_sum, jnp.zeros((6, HD), F32)], 0)
        core = s_ref[1]
        rows = UNIT // 2
        outs[0][...] = acc[pl.ds(pl.multiple_of(core * rows, rows), rows), :]
        outs[1][...] = acc[pl.ds(pl.multiple_of((1 - core) * rows, rows), rows), :]

    shape = jax.ShapeDtypeStruct((UNIT // 2, cols), F32)
    shapes = [shape, shape]
    if with_gains:
        shapes.append(jax.ShapeDtypeStruct((8, HD), F32))
    return call(
        kernel, shapes, [*features] + arrays, 4 * 10**10 if with_gains else 3 * 10**9, scalars,
        scratch=[pltpu.VMEM((UNIT, cols), F32)],
        name="weight_grad_kv" if with_gains else "weight_grad_q",
    )


def gather_near(unit):
    return from_y(unit, 1), from_y(unit, 3), from_x(unit)


def gather_far(unit, near):
    y1, y3, x0 = near
    y2 = from_y(y1, 1)
    x1 = from_y(x0, 1)
    x3 = from_y(x0, 3)
    cut = 2 * TOK
    x2 = [from_y(x1[:cut], 1), from_y(x3[cut:], 3)]
    parts = [[(u, slice(None))] for u in (unit, y1, y3, y2, x0, x1, x3)]
    return parts + [[(u, slice(None)) for u in x2]]


def per_device(
    hidden, w_qkv, norm_gains, upstream, segment_ids, advantages, swap_slot, token_count
):
    data_rank = lax.axis_index("dp")
    shard = lax.axis_index("fsdp")
    core = shard % 2
    chip = shard // 2
    y = chip % 4
    x_hi = chip // 4
    first = core == 0
    slot = swap_slot[jnp.minimum(data_rank, 15 - data_rank)]

    def take(array, index):
        return lax.dynamic_index_in_dim(array, index, 0, keepdims=False)

    first_cols = jnp.concatenate([w_qkv[:, :512], w_qkv[:, 1024:1152]], 1)
    second_cols = jnp.concatenate([w_qkv[:, 512:1024], w_qkv[:, 1152:]], 1)
    mine = jnp.where(first, first_cols, second_cols)
    theirs = core_mate(jnp.where(first, second_cols, first_cols))
    low = jnp.where(first, mine, theirs)
    high = jnp.where(first, theirs, mine)
    unit = jnp.concatenate([low, high], 0)

    place = lambda dx, dy: ((x_hi + dx) % 2) * 4 + (y + dy) % 4
    scalars = jnp.stack(
        [place(1, 2), core, slot, place(0, 0), place(0, 1), place(0, 3), place(0, 2),
         place(1, 0), place(1, 1), place(1, 3)]
    ).astype(jnp.int32)

    ids = jnp.arange(16, dtype=jnp.int32)
    below = jnp.sum((segment_ids[:, :, None] < ids).astype(jnp.int32), 1)
    below = lax.all_to_all(
        jnp.broadcast_to(below[None], (16, 2, 16)), "fsdp", 0, 0, tiled=True
    )
    segments = jnp.stack([segment_ids, core_mate(segment_ids)], 1)
    local = jnp.arange(TOK, dtype=jnp.int32)
    slots = jnp.stack([shard * TOK + local, (shard ^ 1) * TOK + local])[None]
    slots = jnp.broadcast_to(slots, segments.shape)

    def lane_rows(a):
        return jnp.tile(a.reshape(2, 2 * TOK), (1, HEADS))

    lanes = jnp.stack([lane_rows(segments), lane_rows(slots)], 1)
    lanes = jnp.concatenate([lanes, jnp.zeros((2, 6, lanes.shape[-1]), jnp.int32)], 1)
    columns = jnp.concatenate(
        [segments.reshape(4 * TOK, 1), slots.reshape(4 * TOK, 1)], 1
    )

    table = (segment_ids[..., None] == jnp.arange(SEGS, dtype=jnp.int32)).astype(F32)
    per_token = jnp.sum(table * advantages.astype(F32)[:, None, :], -1)
    factor = jnp.float32(2 * 16 * SEQ) / token_count[0].astype(F32)
    cotangent = (upstream.astype(F32) * (per_token * factor)[..., None]).astype(BF16)
    mine_cot = jnp.where(first, cotangent[..., :QCOLS], cotangent[..., QCOLS:])
    other_cot = core_mate(jnp.where(first, cotangent[..., QCOLS:], cotangent[..., :QCOLS]))
    cot = jnp.stack([mine_cot, other_cot], 1)

    rows = [hidden, core_mate(hidden)]
    y1, y3, x0 = from_y(unit, 1), from_y(unit, 3), from_near_x(unit)
    tables = positions(below, lanes, columns, scalars)
    y1, y3, x0 = lax.optimization_barrier((y1, y3, x0))
    y2, x1, x3 = from_y(y1, 1), from_near_x(y1), from_y(x0, 3)
    y2, x1, x3, tables, cot = lax.optimization_barrier((y2, x1, x3, tables, cot))
    cosine_flat, sine_flat, lanes = tables
    cosine = cosine_flat.reshape(2, 2, TOK, HD)
    sine = sine_flat.reshape(2, 2, TOK, HD)
    x2_a, x2_b = from_y(x1[: UNIT // 2], 1), from_y(x3[UNIT // 2 :], 3)
    total = project(rows, [unit, y1, y3, x0], [3, 4, 5, 7], scalars, None)
    total = project(rows, [y2, x1, x3], [6, 8, 9], scalars, total)
    x2_a, x2_b, total = lax.optimization_barrier((x2_a, x2_b, total))
    q, kv, send = project_last(
        rows, [x2_a, x2_b], total, cosine_flat, sine_flat, norm_gains, scalars
    )

    moved = mirror(take(hidden, slot))
    own_rows = jnp.stack([take(hidden, 1 - slot), moved])
    near = lax.dynamic_slice_in_dim(own_rows, (1 - x_hi) * 4 * UNIT, 4 * UNIT, 2)
    near = from_x(after(near, y2, x1, x3))
    blocks = []
    for step in (0, 1, 3, 2):
        to = (y - step) % 4
        blocks.append(
            jnp.stack(
                [
                    lax.dynamic_slice_in_dim(own_rows, (x_hi * 4 + to) * UNIT, UNIT, 2),
                    lax.dynamic_slice_in_dim(near, to * UNIT, UNIT, 2),
                ]
            )
        )

    gathered = chips_exchange(send)
    gathered, blocks = lax.optimization_barrier((gathered, blocks))
    blocks = [blocks[0], from_y(blocks[1], 1), from_y(blocks[2], 3), from_y(blocks[3], 2)]
    kv_shape = (CHIPS, 2, 2, TOK, HD)
    kv_other = core_mate(gathered).reshape(kv_shape)
    kv_mine = gathered.reshape(kv_shape)

    def attend(moved):
        return attention(
            q.reshape(2, 2, TOK, QCOLS), cot, kv_mine, kv_other, lanes, cosine, sine, norm_gains,
            scalars, moved,
        )

    gp_moved, gain_moved, moved_mine, moved_other = attend(True)
    gp_kept, gain_kept, kept_mine, kept_other = attend(False)
    kept_other, blocks, gp_moved = lax.optimization_barrier(
        (kept_other, blocks, mirror(gp_moved))
    )
    gp_q = jnp.concatenate([gp_kept, gp_moved], 0).reshape(4 * TOK, QCOLS)

    summed = jnp.stack(
        [
            moved_mine.astype(F32) + core_mate(moved_other).astype(F32),
            kept_mine.astype(F32) + core_mate(kept_other).astype(F32),
        ],
        1,
    ).astype(BF16)
    terms = chips_exchange(summed.reshape(CHIPS, 2, 2 * TOK, HD))
    near_q = gather_near(gp_q)
    terms = after(terms, *near_q)
    parts_q = gather_far(gp_q, near_q)
    gp_kv = kv_back(
        terms, kv, cosine_flat, sine_flat, norm_gains, (gain_moved, gain_kept), scalars
    )
    gp_kv = jnp.concatenate([gp_kv[1], mirror(gp_kv[0])], 0)
    gp_kv = after(gp_kv, [part[0][0] for part in parts_q[:7]])
    parts_kv = chips_exchange(jnp.broadcast_to(gp_kv[None], (CHIPS, 4 * TOK + 32, HD)))

    pieces = [
        (3, unit), (4, y1), (5, y3), (6, y2), (7, x0), (8, x1), (9, x3), (0, x2_a, x2_b),
    ]
    keep, give = hidden_grad(gp_q, gp_kv, pieces, scalars)
    grad_hidden = (keep + core_mate(give).astype(F32)).astype(BF16).reshape(hidden.shape)

    features = blocks + [core_mate(b) for b in blocks]
    q_mine, q_give = weight_grad(features, parts_q, QCOLS, scalars, False)
    kv_mine, kv_give, gains = weight_grad(
        features, [[(parts_kv, None)]] * CHIPS, HD, scalars, True
    )
    q_got = core_mate(q_give)
    kv_got = core_mate(kv_give)
    grad_weight = jnp.concatenate(
        [
            jnp.where(first, q_mine, q_got), jnp.where(first, q_got, q_mine),
            jnp.where(first, kv_mine, kv_got), jnp.where(first, kv_got, kv_mine),
        ],
        1,
    )
    grad_gains = (gains + core_mate(gains))[:2]
    return (grad_hidden, grad_weight[None], grad_gains[None])


def solution(mesh):
    in_specs = (
        P("dp", "fsdp", None),
        P("fsdp", None),
        P(),
        P("dp", "fsdp", None),
        P("dp", "fsdp"),
        P("dp", None),
        P(),
        P(),
    )
    out_specs = (P("dp", "fsdp", None), P("dp", "fsdp", None), P("dp", None, None))
    return jax.shard_map(
        per_device, mesh=mesh, in_specs=in_specs, out_specs=out_specs, check_vma=False
    )
```

```python
import math

import jax
import jax.numpy as jnp
from jax import lax
from jax.experimental import pallas as pl
from jax.experimental.pallas import tpu as pltpu
from jax.sharding import PartitionSpec as P

HD = 128
HEADS = 4
TOK = 96
CHIPS = 8
UNIT = 640
HALF_COLS = 640
QCOLS = HEADS * HD
SEQ = 1536
SEGS = 8
EPSILON = 1e-06
THETA_LOG = math.log(1000000.0)
SCALING = 1.0 / math.sqrt(HD)
EXP2_SCALE = SCALING * math.log2(math.e)
F32 = jnp.float32
BF16 = jnp.bfloat16
NN = (((1,), (0,)), ((), ()))
NT = (((1,), (1,)), ((), ()))
TN = (((0,), (0,)), ((), ()))
VMEM_LIMIT = 56 * 1024 * 1024


def core_mate(array):
    return lax.ppermute(array, "fsdp", [(i, i ^ 1) for i in range(16)])


def from_y(array, step):
    def there(i):
        return (i & 8) | (((i // 2 - step) % 4) * 2) | (i & 1)

    return lax.ppermute(array, "fsdp", [(i, there(i)) for i in range(16)])


def from_x(array):
    return lax.ppermute(array, "fsdp", [(i, i ^ 8) for i in range(16)])


def from_near_x(array):
    pairs = [(d * 16 + i, (d ^ 8) * 16 + (i ^ 8)) for d in range(16) for i in range(16)]
    return lax.ppermute(array, ("dp", "fsdp"), pairs)


def mirror(array):
    return lax.ppermute(array, "dp", [(i, 15 - i) for i in range(16)])


def chips_exchange(blocks):
    return lax.all_to_all(
        blocks, "fsdp", 0, 0, tiled=True,
        axis_index_groups=[list(range(0, 16, 2)), list(range(1, 16, 2))],
    )


def after(array, *others):
    return lax.optimization_barrier((array, others))[0]


def dot(left, right, dims):
    return lax.dot_general(left, right, dims, preferred_element_type=F32)


def call(kernel, out_shape, arrays, flops, scalars=None, grid=(1,), in_specs=None, out_specs=None,
         scratch=(), name=None):
    whole = lambda s: pl.BlockSpec(s.shape, lambda *_, n=len(s.shape): (0,) * n)
    in_specs = in_specs or [whole(a) for a in arrays]
    outs = out_shape if isinstance(out_shape, (list, tuple)) else [out_shape]
    out_specs = out_specs or [whole(s) for s in outs]
    return pl.pallas_call(
        kernel,
        out_shape=list(outs),
        grid_spec=pltpu.PrefetchScalarGridSpec(
            num_scalar_prefetch=1, grid=grid, in_specs=in_specs, out_specs=out_specs,
            scratch_shapes=list(scratch),
        ),
        compiler_params=pltpu.CompilerParams(vmem_limit_bytes=VMEM_LIMIT),
        cost_estimate=pl.CostEstimate(flops=flops, bytes_accessed=0, transcendentals=0),
        name=name,
    )(scalars, *arrays)


def block_of(place):
    return pl.BlockSpec((2, TOK, UNIT), lambda i, s, j=place: (0, 0, s[j]))


def joined(own, other):
    return jnp.concatenate([own[0], other[0], own[1], other[1]], 0)


def whole_spec(a):
    return pl.BlockSpec(a.shape, lambda *_, n=len(a.shape): (0,) * n)


def project(rows, units, places, scalars, total):
    n = len(units)

    def kernel(s_ref, *refs):
        acc = refs[3 * n][...] if total is not None else None
        for j in range(n):
            term = dot(joined(refs[2 * j], refs[2 * j + 1]), refs[2 * n + j][...], NN)
            acc = term if acc is None else acc + term
        refs[-1][...] = acc

    extra = [] if total is None else [total]
    return call(
        kernel, jax.ShapeDtypeStruct((4 * TOK, HALF_COLS), F32),
        list(rows) * n + units + extra, 0, scalars,
        in_specs=[block_of(j) for j in places for _ in rows]
        + [whole_spec(a) for a in units + extra],
        name="project",
    )[0]


def rotated(x, cosine, sine):
    return x * cosine + pltpu.roll(x, HD // 2, 1) * sine


def unrotated(y, cosine, sine):
    return y * cosine - pltpu.roll(y, HD // 2, 1) * sine


def inverse_rms(x):
    return lax.rsqrt(jnp.mean(x * x, -1, keepdims=True) + EPSILON)


def swap_cores(x):
    return jnp.concatenate([x[i * TOK : (i + 1) * TOK] for i in (1, 0, 3, 2)], 0)


def project_last(rows, unit, total, cosine, sine, gains, scalars):
    def kernel(s_ref, own_ref, other_ref, low_ref, high_ref, total_ref, cos_ref, sin_ref,
               gain_ref, q_ref, kv_ref, send_ref):
        right = jnp.concatenate([low_ref[...], high_ref[...]], 0)
        acc = total_ref[...] + dot(joined(own_ref, other_ref), right, NN)
        q_ref[...] = acc[:, :QCOLS]
        x = acc[:, QCOLS:]
        kv_ref[...] = x

        @pl.when(s_ref[1] == 0)
        def _():
            kn = x * inverse_rms(x) * gain_ref[1:2, :]
            kr = rotated(kn, cos_ref[...], sin_ref[...]).astype(BF16)
            for i in range(CHIPS):
                send_ref[i] = kr

        @pl.when(s_ref[1] != 0)
        def _():
            v = swap_cores(x.astype(BF16))
            for i in range(CHIPS):
                send_ref[i] = v

    arrays = [*rows, *unit, total, cosine, sine, gains]
    shapes = [
        jax.ShapeDtypeStruct((4 * TOK, QCOLS), F32),
        jax.ShapeDtypeStruct((4 * TOK, HD), F32),
        jax.ShapeDtypeStruct((CHIPS, 4 * TOK, HD), BF16),
    ]
    return call(
        kernel, shapes, arrays, 4 * 10**8, scalars,
        in_specs=[block_of(0)] * 2 + [whole_spec(a) for a in arrays[2:]], name="project_last",
    )


def positions(below, tokens, queries, scalars):
    count = 4 * TOK

    def kernel(s_ref, below_ref, tokens_ref, queries_ref, cos_ref, sin_ref, out_ref):
        counts = jnp.sum(below_ref[...], 0)
        lane = lax.broadcasted_iota(jnp.int32, (1, count), 1)
        shard = 2 * s_ref[3] + s_ref[1]
        mate = 2 * s_ref[3] + 1 - s_ref[1]
        slot = jnp.where((lane // TOK) % 2 == 0, shard, mate) * TOK + lane % TOK

        def start_of(seg, pack):
            start = jnp.zeros(seg.shape, jnp.int32)
            for k in range(1, SEGS + 1):
                start = jnp.where(seg == k, counts[pack : pack + 1, k : k + 1], start)
            return start

        seg = tokens_ref[...]
        start = jnp.where(lane < 2 * TOK, start_of(seg, 0), start_of(seg, 1))
        place = jnp.broadcast_to((slot - start).astype(F32), (8, count))
        for p in range(2):
            out_ref[p] = jnp.broadcast_to(slot, (8, count))
            out_ref[p, 0:1, :] = start_of(queries_ref[p : p + 1, :], p)
        half = lax.broadcasted_iota(jnp.int32, (1, HD), 1)
        inverse = jnp.exp(-((half % (HD // 2)).astype(F32) * (2.0 / HD)) * THETA_LOG)
        angles = place.T[:, 0:1] * inverse
        cos_ref[...] = jnp.cos(angles)
        sin_ref[...] = jnp.sin(angles) * jnp.where(half < HD // 2, -1.0, 1.0)

    table = jax.ShapeDtypeStruct((count, HD), F32)
    return call(
        kernel, [table, table, jax.ShapeDtypeStruct((2, 8, count), jnp.int32)],
        [below, tokens, queries], 0, scalars, name="positions",
    )


def attention(q, cotangent, kv_a, kv_b, rows, cosine, sine, gains, scalars, moved):
    chips = 2
    chunk = chips * 2 * TOK
    lanes = HEADS * 2 * TOK
    queries = 2 * TOK

    def kernel(s_ref, q_ref, c_ref, a_ref, b_ref, rows_ref, cos_ref, sin_ref, gain_ref,
               gp_ref, gg_ref, mine_ref, other_ref, k_s, v_s, e_s, d_s):
        first = s_ref[1] == 0

        @pl.when(first)
        def _():
            k_s[...] = a_ref[...].reshape(SEQ, HD)
            v_s[...] = b_ref[...].reshape(SEQ, HD)

        @pl.when(jnp.logical_not(first))
        def _():
            k_s[...] = b_ref[...].reshape(SEQ, HD)
            v_s[...] = a_ref[...].reshape(SEQ, HD)

        cos = cos_ref[...].reshape(queries, HD)
        sin = sin_ref[...].reshape(queries, HD)
        gain = gain_ref[0:1, :]
        q_all = q_ref[...].reshape(queries, QCOLS)
        c_all = c_ref[...].reshape(queries, QCOLS)
        xs = [q_all[:, h * HD : (h + 1) * HD] for h in range(HEADS)]
        rms = [inverse_rms(x) for x in xs]
        qs = jnp.concatenate(
            [rotated(x * r * gain, cos, sin).astype(BF16) for x, r in zip(xs, rms)], 0
        )
        cs = jnp.concatenate([c_all[:, h * HD : (h + 1) * HD] for h in range(HEADS)], 0)
        half = lanes // 2
        start = rows_ref[0, 0:1, :half]
        place = rows_ref[0, 1:2, :half]
        total = jnp.zeros((1, lanes), F32)
        inner = jnp.zeros((1, lanes), F32)
        for c in range(SEQ // chunk):
            at = pl.ds(c * chunk, chunk)
            scores = dot(k_s[at, :], qs, NT)
            u = lax.broadcasted_iota(jnp.int32, (chunk, half), 0) + c * chunk
            seen = jnp.where((u >= start) & (u <= place), 1.0, 0.0)
            e = jnp.exp2(scores * EXP2_SCALE) * jnp.concatenate([seen, seen], 1)
            d = dot(v_s[at, :], cs, NT)
            total = total + jnp.sum(e, 0, keepdims=True)
            inner = inner + jnp.sum(e * d, 0, keepdims=True)
            e_s[at, :] = e
            d_s[at, :] = d
        inverse = 1.0 / total
        inner = inner * inverse
        grad_t = jnp.zeros((HD, lanes), F32)
        for c in range(SEQ // chunk):
            at = pl.ds(c * chunk, chunk)
            p = e_s[at, :] * inverse
            ds = (p * (d_s[at, :] - inner)).astype(BF16)
            dv = dot(p.astype(BF16), cs, NN).astype(BF16).reshape(chips, 2, TOK, HD)
            dk = (dot(ds, qs, NN) * SCALING).astype(BF16).reshape(chips, 2, TOK, HD)
            grad_t = grad_t + dot(k_s[at, :], ds, TN)
            own = pl.ds(c * chips, chips)

            @pl.when(first)
            def _():
                mine_ref[own] = dk
                other_ref[own] = dv

            @pl.when(jnp.logical_not(first))
            def _():
                mine_ref[own] = dv
                other_ref[own] = dk

        grad = grad_t.T * SCALING
        outs = []
        gain_sum = jnp.zeros((1, HD), F32)
        for h in range(HEADS):
            y = unrotated(grad[h * queries : (h + 1) * queries], cos, sin)
            x, r = xs[h], rms[h]
            weighted = y * gain
            mean = jnp.mean(x * weighted, -1, keepdims=True)
            outs.append((r * weighted - x * (r * r * r) * mean).astype(BF16))
            gain_sum = gain_sum + jnp.sum(y * (x * r), 0, keepdims=True)
        gp_ref[...] = jnp.concatenate(outs, 1).reshape(2, TOK, QCOLS)
        gg_ref[...] = jnp.broadcast_to(gain_sum, (8, HD))

    pack = lambda s: s[2] if moved else 1 - s[2]
    token_spec = lambda cols: pl.BlockSpec((1, 2, TOK, cols), lambda i, s: (pack(s), 0, 0, 0))
    kv_spec = pl.BlockSpec((CHIPS, 1, 2, TOK, HD), lambda i, s: (0, pack(s), 0, 0, 0))
    shapes = [
        jax.ShapeDtypeStruct((2, TOK, QCOLS), BF16),
        jax.ShapeDtypeStruct((8, HD), F32),
        jax.ShapeDtypeStruct((CHIPS, 2, TOK, HD), BF16),
        jax.ShapeDtypeStruct((CHIPS, 2, TOK, HD), BF16),
    ]
    return call(
        kernel, shapes, [q, cotangent, kv_a, kv_b, rows, cosine, sine, gains],
        2 * 5 * 2 * SEQ * lanes * HD, scalars,
        in_specs=[
            token_spec(QCOLS), token_spec(QCOLS), kv_spec, kv_spec,
            pl.BlockSpec((1, 8, lanes // 2), lambda i, s: (pack(s), 0, 0)),
            token_spec(HD), token_spec(HD), whole_spec(gains),
        ],
        scratch=[
            pltpu.VMEM((SEQ, HD), BF16), pltpu.VMEM((SEQ, HD), BF16),
            pltpu.VMEM((SEQ, lanes), F32), pltpu.VMEM((SEQ, lanes), F32),
        ],
        name="attention",
    )


def kv_back(terms, kv, cosine, sine, gains, gain_parts, scalars):
    rows = 2 * TOK

    def kernel(s_ref, t_ref, kv_ref, cos_ref, sin_ref, gain_ref, moved_ref, kept_ref, out_ref):
        grad = t_ref[0, 0].astype(F32)
        for i in range(1, CHIPS):
            grad = grad + t_ref[i, 0].astype(F32)
        q_sum = jnp.where(pl.program_id(0) == 0, moved_ref[0:1, :], kept_ref[0:1, :])

        def put(values, key_sum):
            parts = []
            for s in (q_sum, key_sum):
                high = s.astype(BF16)
                rest = s - high.astype(F32)
                middle = rest.astype(BF16)
                parts += [high.astype(F32), middle.astype(F32), rest - middle.astype(F32)]
            parts.append(jnp.zeros((16 - len(parts), HD), F32))
            out_ref[0, :rows, :] = values
            out_ref[0, rows:, :] = jnp.concatenate(parts, 0).astype(BF16)

        @pl.when(s_ref[1] == 0)
        def _():
            y = unrotated(grad, cos_ref[...], sin_ref[...])
            x = kv_ref[...]
            r = inverse_rms(x)
            weighted = y * gain_ref[1:2, :]
            mean = jnp.mean(x * weighted, -1, keepdims=True)
            values = (r * weighted - x * (r * r * r) * mean).astype(BF16)
            put(values, jnp.sum(y * (x * r), 0, keepdims=True))

        @pl.when(s_ref[1] != 0)
        def _():
            values = grad.astype(BF16)
            put(jnp.concatenate([values[TOK:], values[:TOK]], 0), jnp.zeros((1, HD), F32))

    pack_spec = pl.BlockSpec((rows, HD), lambda p, s: (s[2] + p - 2 * s[2] * p, 0))
    arrays = [terms, kv, cosine, sine, gains, *gain_parts]
    return call(
        kernel, jax.ShapeDtypeStruct((2, rows + 16, HD), BF16), arrays, 0, scalars, grid=(2,),
        in_specs=[pl.BlockSpec((CHIPS, 1, rows, HD), lambda p, s: (0, p, 0, 0))]
        + [pack_spec] * 3 + [whole_spec(a) for a in arrays[4:]],
        out_specs=[pl.BlockSpec((1, rows + 16, HD), lambda p, s: (p, 0, 0))],
        name="kv_back",
    )[0]


def hidden_grad(gp_q, gp_kv, units, scalars):
    def kernel(s_ref, q_ref, kv_ref, *refs):
        keep_ref, send_ref = refs[-2:]
        keys = jnp.concatenate([kv_ref[: 2 * TOK, :], kv_ref[2 * TOK + 16 : 4 * TOK + 16, :]], 0)
        left = jnp.concatenate([q_ref[...], keys], 1)
        refs = list(refs)
        for place, *pieces in units:
            col = pl.multiple_of(s_ref[place] * UNIT, 128)
            unit = jnp.concatenate([refs.pop(0)[...] for _ in pieces], 0)
            out = dot(left, unit, NT)
            for i in range(2):
                slot = s_ref[2] if i else 1 - s_ref[2]
                at = (pl.ds(pl.multiple_of(slot * TOK, TOK), TOK), pl.ds(col, UNIT))
                keep_ref[at] = out[2 * i * TOK : (2 * i + 1) * TOK]
                send_ref[at] = out[(2 * i + 1) * TOK : (2 * i + 2) * TOK].astype(BF16)

    shapes = [
        jax.ShapeDtypeStruct((2 * TOK, CHIPS * UNIT), F32),
        jax.ShapeDtypeStruct((2 * TOK, CHIPS * UNIT), BF16),
    ]
    return call(
        kernel, shapes, [gp_q, gp_kv] + [p for u in units for p in u[1:]],
        3 * 10**9, scalars, name="hidden_grad",
    )


def weight_grad(features, parts, cols, scalars, with_gains):
    arrays, index = [], []
    for part in parts:
        for a, at in part:
            if not any(a is b for b in arrays):
                arrays.append(a)
        index.append([(next(i for i, b in enumerate(arrays) if a is b), at) for a, at in part])

    def kernel(s_ref, *refs):
        places = (3, 4, 5, 6, 7, 8, 9, 0)
        feature_refs, refs = refs[:8], refs[8:]
        acc = refs[-1]
        total = None
        gains = None
        for j in range(0, CHIPS, 2):
            left, right = [], []
            for i in (j, j + 1):
                own, other = feature_refs[i % 4], feature_refs[4 + i % 4]
                left += [f[i // 4, pack] for pack in range(2) for f in (own, other)]
                rows = [refs[a][s_ref[places[i]] if at is None else at] for a, at in index[i]]
                if with_gains:
                    half = 2 * TOK + 16
                    part = rows[0][half - 16 : half].astype(F32)
                    part = part + rows[0][2 * half - 16 :].astype(F32)
                    gains = part if gains is None else gains + part
                    rows = [rows[0][: half - 16], rows[0][half : 2 * half - 16]]
                right += rows
            left, right = jnp.concatenate(left, 0), jnp.concatenate(right, 0)
            if with_gains:
                term = dot(right, left, TN)
                total = term if total is None else total + term
            elif j == 0:
                acc[...] = dot(left, right, TN)
            else:
                acc[...] += dot(left, right, TN)
        outs = refs[len(arrays) : -1]
        if with_gains:
            acc[...] = total.T
            q_sum = gains[0:1] + gains[1:2] + gains[2:3]
            k_sum = gains[3:4] + gains[4:5] + gains[5:6]
            outs[2][...] = jnp.concatenate([q_sum, k_sum, jnp.zeros((6, HD), F32)], 0)
        core = s_ref[1]
        rows = UNIT // 2
        outs[0][...] = acc[pl.ds(pl.multiple_of(core * rows, rows), rows), :]
        outs[1][...] = acc[pl.ds(pl.multiple_of((1 - core) * rows, rows), rows), :]

    shape = jax.ShapeDtypeStruct((UNIT // 2, cols), F32)
    shapes = [shape, shape]
    if with_gains:
        shapes.append(jax.ShapeDtypeStruct((8, HD), F32))
    return call(
        kernel, shapes, [*features] + arrays, 4 * 10**10 if with_gains else 3 * 10**9, scalars,
        scratch=[pltpu.VMEM((UNIT, cols), F32)],
        name="weight_grad_kv" if with_gains else "weight_grad_q",
    )


def gather_near(unit):
    return from_y(unit, 1), from_y(unit, 3), from_x(unit)


def gather_far(unit, near):
    y1, y3, x0 = near
    y2 = from_y(y1, 1)
    x1 = from_y(x0, 1)
    x3 = from_y(x0, 3)
    cut = 2 * TOK
    x2 = [from_y(x1[:cut], 1), from_y(x3[cut:], 3)]
    parts = [[(u, slice(None))] for u in (unit, y1, y3, y2, x0, x1, x3)]
    return parts + [[(u, slice(None)) for u in x2]]


def per_device(
    hidden, w_qkv, norm_gains, upstream, segment_ids, advantages, swap_slot, token_count
):
    data_rank = lax.axis_index("dp")
    shard = lax.axis_index("fsdp")
    core = shard % 2
    chip = shard // 2
    y = chip % 4
    x_hi = chip // 4
    first = core == 0
    slot = swap_slot[jnp.minimum(data_rank, 15 - data_rank)]

    def take(array, index):
        return lax.dynamic_index_in_dim(array, index, 0, keepdims=False)

    first_cols = jnp.concatenate([w_qkv[:, :512], w_qkv[:, 1024:1152]], 1)
    second_cols = jnp.concatenate([w_qkv[:, 512:1024], w_qkv[:, 1152:]], 1)
    mine = jnp.where(first, first_cols, second_cols)
    theirs = core_mate(jnp.where(first, second_cols, first_cols))
    low = jnp.where(first, mine, theirs)
    high = jnp.where(first, theirs, mine)
    unit = jnp.concatenate([low, high], 0)

    place = lambda dx, dy: ((x_hi + dx) % 2) * 4 + (y + dy) % 4
    scalars = jnp.stack(
        [place(1, 2), core, slot, place(0, 0), place(0, 1), place(0, 3), place(0, 2),
         place(1, 0), place(1, 1), place(1, 3)]
    ).astype(jnp.int32)

    ids = jnp.arange(16, dtype=jnp.int32)
    below = jnp.sum((segment_ids[:, :, None] < ids).astype(jnp.int32), 1)
    below = lax.all_to_all(
        jnp.broadcast_to(below[None], (16, 2, 16)), "fsdp", 0, 0, tiled=True
    )
    mate_ids = core_mate(segment_ids)
    both = [segment_ids[0:1], mate_ids[0:1], segment_ids[1:2], mate_ids[1:2]]
    tokens = jnp.concatenate(both, 1)
    queries = jnp.concatenate([segment_ids, mate_ids, segment_ids, mate_ids], 1)

    table = (segment_ids[..., None] == jnp.arange(SEGS, dtype=jnp.int32)).astype(F32)
    per_token = jnp.sum(table * advantages.astype(F32)[:, None, :], -1)
    factor = jnp.float32(2 * 16 * SEQ) / token_count[0].astype(F32)
    cotangent = (upstream.astype(F32) * (per_token * factor)[..., None]).astype(BF16)
    mine_cot = jnp.where(first, cotangent[..., :QCOLS], cotangent[..., QCOLS:])
    other_cot = core_mate(jnp.where(first, cotangent[..., QCOLS:], cotangent[..., :QCOLS]))
    cot = jnp.stack([mine_cot, other_cot], 1)

    rows = [hidden, core_mate(hidden)]
    y1, y3, x0 = from_y(unit, 1), from_y(unit, 3), from_near_x(unit)
    tables = positions(below, tokens, queries, scalars)
    y1, y3, x0 = lax.optimization_barrier((y1, y3, x0))
    y2, x1, x3 = from_y(y1, 1), from_near_x(y1), from_y(x0, 3)
    y2, x1, x3, tables, cot = lax.optimization_barrier((y2, x1, x3, tables, cot))
    cosine_flat, sine_flat, lanes = tables
    cosine = cosine_flat.reshape(2, 2, TOK, HD)
    sine = sine_flat.reshape(2, 2, TOK, HD)
    x2_a, x2_b = from_y(x1[: UNIT // 2], 1), from_y(x3[UNIT // 2 :], 3)
    total = project(rows, [unit, y1, y3, x0], [3, 4, 5, 7], scalars, None)
    total = project(rows, [y2, x1, x3], [6, 8, 9], scalars, total)
    x2_a, x2_b, total = lax.optimization_barrier((x2_a, x2_b, total))
    q, kv, send = project_last(
        rows, [x2_a, x2_b], total, cosine_flat, sine_flat, norm_gains, scalars
    )

    moved = mirror(take(hidden, slot))
    own_rows = jnp.stack([take(hidden, 1 - slot), moved])
    near = lax.dynamic_slice_in_dim(own_rows, (1 - x_hi) * 4 * UNIT, 4 * UNIT, 2)
    near = from_x(after(near, y2, x1, x3))
    blocks = []
    for step in (0, 1, 3, 2):
        to = (y - step) % 4
        blocks.append(
            jnp.stack(
                [
                    lax.dynamic_slice_in_dim(own_rows, (x_hi * 4 + to) * UNIT, UNIT, 2),
                    lax.dynamic_slice_in_dim(near, to * UNIT, UNIT, 2),
                ]
            )
        )

    gathered = chips_exchange(send)
    gathered, blocks = lax.optimization_barrier((gathered, blocks))
    blocks = [blocks[0], from_y(blocks[1], 1), from_y(blocks[2], 3), from_y(blocks[3], 2)]
    kv_shape = (CHIPS, 2, 2, TOK, HD)
    kv_other = core_mate(gathered).reshape(kv_shape)
    kv_mine = gathered.reshape(kv_shape)

    def attend(moved):
        return attention(
            q.reshape(2, 2, TOK, QCOLS), cot, kv_mine, kv_other, lanes, cosine, sine, norm_gains,
            scalars, moved,
        )

    gp_moved, gain_moved, moved_mine, moved_other = attend(True)
    gp_kept, gain_kept, kept_mine, kept_other = attend(False)
    kept_other, blocks, gp_moved = lax.optimization_barrier(
        (kept_other, blocks, mirror(gp_moved))
    )
    gp_q = jnp.concatenate([gp_kept, gp_moved], 0).reshape(4 * TOK, QCOLS)

    summed = jnp.stack(
        [
            moved_mine.astype(F32) + core_mate(moved_other).astype(F32),
            kept_mine.astype(F32) + core_mate(kept_other).astype(F32),
        ],
        1,
    ).astype(BF16)
    terms = chips_exchange(summed.reshape(CHIPS, 2, 2 * TOK, HD))
    near_q = gather_near(gp_q)
    parts_q = gather_far(gp_q, near_q)
    gp_kv = kv_back(
        terms, kv, cosine_flat, sine_flat, norm_gains, (gain_moved, gain_kept), scalars
    )
    gp_kv = jnp.concatenate([gp_kv[1], mirror(gp_kv[0])], 0)
    gp_kv = after(gp_kv, [part[0][0] for part in parts_q[:7]])
    parts_kv = chips_exchange(jnp.broadcast_to(gp_kv[None], (CHIPS, 4 * TOK + 32, HD)))

    pieces = [
        (3, unit), (4, y1), (5, y3), (6, y2), (7, x0), (8, x1), (9, x3), (0, x2_a, x2_b),
    ]
    keep, give = hidden_grad(gp_q, gp_kv, pieces, scalars)
    grad_hidden = (keep + core_mate(give).astype(F32)).astype(BF16).reshape(hidden.shape)

    features = blocks + [core_mate(b) for b in blocks]
    q_mine, q_give = weight_grad(features, parts_q, QCOLS, scalars, False)
    kv_mine, kv_give, gains = weight_grad(
        features, [[(parts_kv, None)]] * CHIPS, HD, scalars, True
    )
    q_got = core_mate(q_give)
    kv_got = core_mate(kv_give)
    grad_weight = jnp.concatenate(
        [
            jnp.where(first, q_mine, q_got), jnp.where(first, q_got, q_mine),
            jnp.where(first, kv_mine, kv_got), jnp.where(first, kv_got, kv_mine),
        ],
        1,
    )
    grad_gains = (gains + core_mate(gains))[:2]
    return (grad_hidden, grad_weight[None], grad_gains[None])


def solution(mesh):
    in_specs = (
        P("dp", "fsdp", None),
        P("fsdp", None),
        P(),
        P("dp", "fsdp", None),
        P("dp", "fsdp"),
        P("dp", None),
        P(),
        P(),
    )
    out_specs = (P("dp", "fsdp", None), P("dp", "fsdp", None), P("dp", None, None))
    return jax.shard_map(
        per_device, mesh=mesh, in_specs=in_specs, out_specs=out_specs, check_vma=False
    )
```

```python
import math

import jax
import jax.numpy as jnp
from jax import lax
from jax.experimental import pallas as pl
from jax.experimental.pallas import tpu as pltpu
from jax.sharding import PartitionSpec as P

HD = 128
HEADS = 4
TOK = 96
CHIPS = 8
UNIT = 640
HALF_COLS = 640
QCOLS = HEADS * HD
SEQ = 1536
SEGS = 8
EPSILON = 1e-06
THETA_LOG = math.log(1000000.0)
SCALING = 1.0 / math.sqrt(HD)
EXP2_SCALE = SCALING * math.log2(math.e)
F32 = jnp.float32
BF16 = jnp.bfloat16
NN = (((1,), (0,)), ((), ()))
NT = (((1,), (1,)), ((), ()))
TN = (((0,), (0,)), ((), ()))
VMEM_LIMIT = 56 * 1024 * 1024


def core_mate(array):
    return lax.ppermute(array, "fsdp", [(i, i ^ 1) for i in range(16)])


def from_y(array, step):
    def there(i):
        return (i & 8) | (((i // 2 - step) % 4) * 2) | (i & 1)

    return lax.ppermute(array, "fsdp", [(i, there(i)) for i in range(16)])


def from_x(array):
    return lax.ppermute(array, "fsdp", [(i, i ^ 8) for i in range(16)])


def from_near_x(array):
    pairs = [(d * 16 + i, (d ^ 8) * 16 + (i ^ 8)) for d in range(16) for i in range(16)]
    return lax.ppermute(array, ("dp", "fsdp"), pairs)


def mirror(array):
    return lax.ppermute(array, "dp", [(i, 15 - i) for i in range(16)])


def chips_exchange(blocks):
    return lax.all_to_all(
        blocks, "fsdp", 0, 0, tiled=True,
        axis_index_groups=[list(range(0, 16, 2)), list(range(1, 16, 2))],
    )


def after(array, *others):
    return lax.optimization_barrier((array, others))[0]


def dot(left, right, dims):
    return lax.dot_general(left, right, dims, preferred_element_type=F32)


def call(kernel, out_shape, arrays, flops, scalars=None, grid=(1,), in_specs=None, out_specs=None,
         scratch=(), name=None):
    whole = lambda s: pl.BlockSpec(s.shape, lambda *_, n=len(s.shape): (0,) * n)
    in_specs = in_specs or [whole(a) for a in arrays]
    outs = out_shape if isinstance(out_shape, (list, tuple)) else [out_shape]
    out_specs = out_specs or [whole(s) for s in outs]
    return pl.pallas_call(
        kernel,
        out_shape=list(outs),
        grid_spec=pltpu.PrefetchScalarGridSpec(
            num_scalar_prefetch=1, grid=grid, in_specs=in_specs, out_specs=out_specs,
            scratch_shapes=list(scratch),
        ),
        compiler_params=pltpu.CompilerParams(vmem_limit_bytes=VMEM_LIMIT),
        cost_estimate=pl.CostEstimate(flops=flops, bytes_accessed=0, transcendentals=0),
        name=name,
    )(scalars, *arrays)


def block_of(place):
    return pl.BlockSpec((2, TOK, UNIT), lambda i, s, j=place: (0, 0, s[j]))


def joined(own, other):
    return jnp.concatenate([own[0], other[0], own[1], other[1]], 0)


def whole_spec(a):
    return pl.BlockSpec(a.shape, lambda *_, n=len(a.shape): (0,) * n)


def project(rows, units, places, scalars, total):
    n = len(units)

    def kernel(s_ref, *refs):
        acc = refs[3 * n][...] if total is not None else None
        for j in range(n):
            term = dot(joined(refs[2 * j], refs[2 * j + 1]), refs[2 * n + j][...], NN)
            acc = term if acc is None else acc + term
        refs[-1][...] = acc

    extra = [] if total is None else [total]
    return call(
        kernel, jax.ShapeDtypeStruct((4 * TOK, HALF_COLS), F32),
        list(rows) * n + units + extra, 0, scalars,
        in_specs=[block_of(j) for j in places for _ in rows]
        + [whole_spec(a) for a in units + extra],
        name="project",
    )[0]


def rotated(x, cosine, sine):
    return x * cosine + pltpu.roll(x, HD // 2, 1) * sine


def unrotated(y, cosine, sine):
    return y * cosine - pltpu.roll(y, HD // 2, 1) * sine


def inverse_rms(x):
    return lax.rsqrt(jnp.mean(x * x, -1, keepdims=True) + EPSILON)


def swap_cores(x):
    return jnp.concatenate([x[i * TOK : (i + 1) * TOK] for i in (1, 0, 3, 2)], 0)


def project_last(rows, unit, total, cosine, sine, gains, scalars):
    def kernel(s_ref, own_ref, other_ref, low_ref, high_ref, total_ref, cos_ref, sin_ref,
               gain_ref, q_ref, kv_ref, send_ref):
        right = jnp.concatenate([low_ref[...], high_ref[...]], 0)
        acc = total_ref[...] + dot(joined(own_ref, other_ref), right, NN)
        q_ref[...] = acc[:, :QCOLS]
        x = acc[:, QCOLS:]
        kv_ref[...] = x

        @pl.when(s_ref[1] == 0)
        def _():
            kn = x * inverse_rms(x) * gain_ref[1:2, :]
            kr = rotated(kn, cos_ref[...], sin_ref[...]).astype(BF16)
            for i in range(CHIPS):
                send_ref[i] = kr

        @pl.when(s_ref[1] != 0)
        def _():
            v = swap_cores(x.astype(BF16))
            for i in range(CHIPS):
                send_ref[i] = v

    arrays = [*rows, *unit, total, cosine, sine, gains]
    shapes = [
        jax.ShapeDtypeStruct((4 * TOK, QCOLS), F32),
        jax.ShapeDtypeStruct((4 * TOK, HD), F32),
        jax.ShapeDtypeStruct((CHIPS, 4 * TOK, HD), BF16),
    ]
    return call(
        kernel, shapes, arrays, 4 * 10**8, scalars,
        in_specs=[block_of(0)] * 2 + [whole_spec(a) for a in arrays[2:]], name="project_last",
    )


def positions(below, tokens, queries, scalars):
    count = 4 * TOK

    def kernel(s_ref, below_ref, tokens_ref, queries_ref, cos_ref, sin_ref, out_ref):
        counts = jnp.sum(below_ref[...], 0)
        lane = lax.broadcasted_iota(jnp.int32, (1, count), 1)
        shard = 2 * s_ref[3] + s_ref[1]
        mate = 2 * s_ref[3] + 1 - s_ref[1]
        slot = jnp.where((lane // TOK) % 2 == 0, shard, mate) * TOK + lane % TOK

        def start_of(seg, pack):
            start = jnp.zeros(seg.shape, jnp.int32)
            for k in range(1, SEGS + 1):
                start = jnp.where(seg == k, counts[pack : pack + 1, k : k + 1], start)
            return start

        seg = tokens_ref[...]
        start = jnp.where(lane < 2 * TOK, start_of(seg, 0), start_of(seg, 1))
        place = jnp.broadcast_to((slot - start).astype(F32), (8, count))
        for p in range(2):
            out_ref[p] = jnp.broadcast_to(slot, (8, count))
            out_ref[p, 0:1, :] = start_of(queries_ref[p : p + 1, :], p)
        half = lax.broadcasted_iota(jnp.int32, (1, HD), 1)
        inverse = jnp.exp(-((half % (HD // 2)).astype(F32) * (2.0 / HD)) * THETA_LOG)
        angles = place.T[:, 0:1] * inverse
        cos_ref[...] = jnp.cos(angles)
        sin_ref[...] = jnp.sin(angles) * jnp.where(half < HD // 2, -1.0, 1.0)

    table = jax.ShapeDtypeStruct((count, HD), F32)
    return call(
        kernel, [table, table, jax.ShapeDtypeStruct((2, 8, count), jnp.int32)],
        [below, tokens, queries], 0, scalars, name="positions",
    )


def attention(q, cotangent, kv_a, kv_b, rows, cosine, sine, gains, scalars, moved):
    chips = 2
    chunk = chips * 2 * TOK
    lanes = HEADS * 2 * TOK
    queries = 2 * TOK

    def kernel(s_ref, q_ref, c_ref, a_ref, b_ref, rows_ref, cos_ref, sin_ref, gain_ref,
               gp_ref, gg_ref, mine_ref, other_ref, k_s, v_s, e_s, d_s):
        first = s_ref[1] == 0

        @pl.when(first)
        def _():
            k_s[...] = a_ref[...].reshape(SEQ, HD)
            v_s[...] = b_ref[...].reshape(SEQ, HD)

        @pl.when(jnp.logical_not(first))
        def _():
            k_s[...] = b_ref[...].reshape(SEQ, HD)
            v_s[...] = a_ref[...].reshape(SEQ, HD)

        cos = cos_ref[...].reshape(queries, HD)
        sin = sin_ref[...].reshape(queries, HD)
        gain = gain_ref[0:1, :]
        q_all = q_ref[...].reshape(queries, QCOLS)
        c_all = c_ref[...].reshape(queries, QCOLS)
        xs = [q_all[:, h * HD : (h + 1) * HD] for h in range(HEADS)]
        rms = [inverse_rms(x) for x in xs]
        qs = jnp.concatenate(
            [rotated(x * r * gain, cos, sin).astype(BF16) for x, r in zip(xs, rms)], 0
        )
        cs = jnp.concatenate([c_all[:, h * HD : (h + 1) * HD] for h in range(HEADS)], 0)
        half = lanes // 2
        start = rows_ref[0, 0:1, :half]
        place = rows_ref[0, 1:2, :half]
        total = jnp.zeros((1, lanes), F32)
        inner = jnp.zeros((1, lanes), F32)
        for c in range(SEQ // chunk):
            at = pl.ds(c * chunk, chunk)
            scores = dot(k_s[at, :], qs, NT)
            u = lax.broadcasted_iota(jnp.int32, (chunk, half), 0) + c * chunk
            seen = jnp.where((u >= start) & (u <= place), 1.0, 0.0)
            e = jnp.exp2(scores * EXP2_SCALE) * jnp.concatenate([seen, seen], 1)
            d = dot(v_s[at, :], cs, NT)
            total = total + jnp.sum(e, 0, keepdims=True)
            inner = inner + jnp.sum(e * d, 0, keepdims=True)
            e_s[at, :] = e
            d_s[at, :] = d
        inverse = 1.0 / total
        inner = inner * inverse
        grad_t = jnp.zeros((HD, lanes), F32)
        for c in range(SEQ // chunk):
            at = pl.ds(c * chunk, chunk)
            p = e_s[at, :] * inverse
            ds = (p * (d_s[at, :] - inner)).astype(BF16)
            dv = dot(p.astype(BF16), cs, NN).astype(BF16).reshape(chips, 2, TOK, HD)
            dk = (dot(ds, qs, NN) * SCALING).astype(BF16).reshape(chips, 2, TOK, HD)
            grad_t = grad_t + dot(k_s[at, :], ds, TN)
            own = pl.ds(c * chips, chips)

            @pl.when(first)
            def _():
                mine_ref[own] = dk
                other_ref[own] = dv

            @pl.when(jnp.logical_not(first))
            def _():
                mine_ref[own] = dv
                other_ref[own] = dk

        grad = grad_t.T * SCALING
        outs = []
        gain_sum = jnp.zeros((1, HD), F32)
        for h in range(HEADS):
            y = unrotated(grad[h * queries : (h + 1) * queries], cos, sin)
            x, r = xs[h], rms[h]
            weighted = y * gain
            mean = jnp.mean(x * weighted, -1, keepdims=True)
            outs.append((r * weighted - x * (r * r * r) * mean).astype(BF16))
            gain_sum = gain_sum + jnp.sum(y * (x * r), 0, keepdims=True)
        gp_ref[...] = jnp.concatenate(outs, 1).reshape(2, TOK, QCOLS)
        gg_ref[...] = jnp.broadcast_to(gain_sum, (8, HD))

    pack = lambda s: s[2] if moved else 1 - s[2]
    token_spec = lambda cols: pl.BlockSpec((1, 2, TOK, cols), lambda i, s: (pack(s), 0, 0, 0))
    kv_spec = pl.BlockSpec((CHIPS, 1, 2, TOK, HD), lambda i, s: (0, pack(s), 0, 0, 0))
    shapes = [
        jax.ShapeDtypeStruct((2, TOK, QCOLS), BF16),
        jax.ShapeDtypeStruct((8, HD), F32),
        jax.ShapeDtypeStruct((CHIPS, 2, TOK, HD), BF16),
        jax.ShapeDtypeStruct((CHIPS, 2, TOK, HD), BF16),
    ]
    return call(
        kernel, shapes, [q, cotangent, kv_a, kv_b, rows, cosine, sine, gains],
        2 * 5 * 2 * SEQ * lanes * HD, scalars,
        in_specs=[
            token_spec(QCOLS), token_spec(QCOLS), kv_spec, kv_spec,
            pl.BlockSpec((1, 8, lanes // 2), lambda i, s: (pack(s), 0, 0)),
            token_spec(HD), token_spec(HD), whole_spec(gains),
        ],
        scratch=[
            pltpu.VMEM((SEQ, HD), BF16), pltpu.VMEM((SEQ, HD), BF16),
            pltpu.VMEM((SEQ, lanes), F32), pltpu.VMEM((SEQ, lanes), F32),
        ],
        name="attention",
    )


def kv_back(terms, kv, cosine, sine, gains, gain_parts, scalars):
    rows = 2 * TOK

    def kernel(s_ref, t_ref, kv_ref, cos_ref, sin_ref, gain_ref, moved_ref, kept_ref, out_ref):
        grad = t_ref[0, 0].astype(F32)
        for i in range(1, CHIPS):
            grad = grad + t_ref[i, 0].astype(F32)
        q_sum = jnp.where(pl.program_id(0) == 0, moved_ref[0:1, :], kept_ref[0:1, :])

        def put(values, key_sum):
            parts = []
            for s in (q_sum, key_sum):
                high = s.astype(BF16)
                rest = s - high.astype(F32)
                middle = rest.astype(BF16)
                parts += [high.astype(F32), middle.astype(F32), rest - middle.astype(F32)]
            parts.append(jnp.zeros((16 - len(parts), HD), F32))
            out_ref[0, :rows, :] = values
            out_ref[0, rows:, :] = jnp.concatenate(parts, 0).astype(BF16)

        @pl.when(s_ref[1] == 0)
        def _():
            y = unrotated(grad, cos_ref[...], sin_ref[...])
            x = kv_ref[...]
            r = inverse_rms(x)
            weighted = y * gain_ref[1:2, :]
            mean = jnp.mean(x * weighted, -1, keepdims=True)
            values = (r * weighted - x * (r * r * r) * mean).astype(BF16)
            put(values, jnp.sum(y * (x * r), 0, keepdims=True))

        @pl.when(s_ref[1] != 0)
        def _():
            values = grad.astype(BF16)
            put(jnp.concatenate([values[TOK:], values[:TOK]], 0), jnp.zeros((1, HD), F32))

    pack_spec = pl.BlockSpec((rows, HD), lambda p, s: (s[2] + p - 2 * s[2] * p, 0))
    arrays = [terms, kv, cosine, sine, gains, *gain_parts]
    return call(
        kernel, jax.ShapeDtypeStruct((2, rows + 16, HD), BF16), arrays, 0, scalars, grid=(2,),
        in_specs=[pl.BlockSpec((CHIPS, 1, rows, HD), lambda p, s: (0, p, 0, 0))]
        + [pack_spec] * 3 + [whole_spec(a) for a in arrays[4:]],
        out_specs=[pl.BlockSpec((1, rows + 16, HD), lambda p, s: (p, 0, 0))],
        name="kv_back",
    )[0]


def hidden_grad(gp_q, gp_kv, units, scalars):
    def kernel(s_ref, q_ref, kv_ref, *refs):
        keep_ref, send_ref = refs[-2:]
        keys = jnp.concatenate([kv_ref[: 2 * TOK, :], kv_ref[2 * TOK + 16 : 4 * TOK + 16, :]], 0)
        left = jnp.concatenate([q_ref[...], keys], 1)
        refs = list(refs)
        for place, *pieces in units:
            col = pl.multiple_of(s_ref[place] * UNIT, 128)
            unit = jnp.concatenate([refs.pop(0)[...] for _ in pieces], 0)
            out = dot(left, unit, NT)
            for i in range(2):
                slot = s_ref[2] if i else 1 - s_ref[2]
                at = (pl.ds(pl.multiple_of(slot * TOK, TOK), TOK), pl.ds(col, UNIT))
                keep_ref[at] = out[2 * i * TOK : (2 * i + 1) * TOK]
                send_ref[at] = out[(2 * i + 1) * TOK : (2 * i + 2) * TOK].astype(BF16)

    shapes = [
        jax.ShapeDtypeStruct((2 * TOK, CHIPS * UNIT), F32),
        jax.ShapeDtypeStruct((2 * TOK, CHIPS * UNIT), BF16),
    ]
    return call(
        kernel, shapes, [gp_q, gp_kv] + [p for u in units for p in u[1:]],
        3 * 10**9, scalars, name="hidden_grad",
    )


def weight_grad(features, parts, cols, scalars, with_gains):
    arrays, index = [], []
    for part in parts:
        for a, at in part:
            if not any(a is b for b in arrays):
                arrays.append(a)
        index.append([(next(i for i, b in enumerate(arrays) if a is b), at) for a, at in part])

    def kernel(s_ref, *refs):
        places = (3, 4, 5, 6, 7, 8, 9, 0)
        feature_refs, refs = refs[:8], refs[8:]
        acc = refs[-1]
        total = None
        gains = None
        for j in range(0, CHIPS, 2):
            left, right = [], []
            for i in (j, j + 1):
                own, other = feature_refs[i % 4], feature_refs[4 + i % 4]
                left += [f[i // 4, pack] for pack in range(2) for f in (own, other)]
                rows = [refs[a][s_ref[places[i]] if at is None else at] for a, at in index[i]]
                if with_gains:
                    half = 2 * TOK + 16
                    part = rows[0][half - 16 : half].astype(F32)
                    part = part + rows[0][2 * half - 16 :].astype(F32)
                    gains = part if gains is None else gains + part
                    rows = [rows[0][: half - 16], rows[0][half : 2 * half - 16]]
                right += rows
            left, right = jnp.concatenate(left, 0), jnp.concatenate(right, 0)
            if with_gains:
                term = dot(right, left, TN)
                total = term if total is None else total + term
            elif j == 0:
                acc[...] = dot(left, right, TN)
            else:
                acc[...] += dot(left, right, TN)
        outs = refs[len(arrays) : -1]
        if with_gains:
            acc[...] = total.T
            q_sum = gains[0:1] + gains[1:2] + gains[2:3]
            k_sum = gains[3:4] + gains[4:5] + gains[5:6]
            outs[2][...] = jnp.concatenate([q_sum, k_sum, jnp.zeros((6, HD), F32)], 0)
        core = s_ref[1]
        rows = UNIT // 2
        outs[0][...] = acc[pl.ds(pl.multiple_of(core * rows, rows), rows), :]
        outs[1][...] = acc[pl.ds(pl.multiple_of((1 - core) * rows, rows), rows), :]

    shape = jax.ShapeDtypeStruct((UNIT // 2, cols), F32)
    shapes = [shape, shape]
    if with_gains:
        shapes.append(jax.ShapeDtypeStruct((8, HD), F32))
    return call(
        kernel, shapes, [*features] + arrays, 4 * 10**10 if with_gains else 3 * 10**9, scalars,
        scratch=[pltpu.VMEM((UNIT, cols), F32)],
        name="weight_grad_kv" if with_gains else "weight_grad_q",
    )


def gather_near(unit):
    return from_y(unit, 1), from_y(unit, 3), from_x(unit)


def gather_far(unit, near):
    y1, y3, x0 = near
    y2 = from_y(y1, 1)
    x1 = from_y(x0, 1)
    x3 = from_y(x0, 3)
    cut = 2 * TOK
    x2 = [from_y(x1[:cut], 1), from_y(x3[cut:], 3)]
    parts = [[(u, slice(None))] for u in (unit, y1, y3, y2, x0, x1, x3)]
    return parts + [[(u, slice(None)) for u in x2]]


def per_device(
    hidden, w_qkv, norm_gains, upstream, segment_ids, advantages, swap_slot, token_count
):
    data_rank = lax.axis_index("dp")
    shard = lax.axis_index("fsdp")
    core = shard % 2
    chip = shard // 2
    y = chip % 4
    x_hi = chip // 4
    first = core == 0
    slot = swap_slot[jnp.minimum(data_rank, 15 - data_rank)]

    def take(array, index):
        return lax.dynamic_index_in_dim(array, index, 0, keepdims=False)

    first_cols = jnp.concatenate([w_qkv[:, :512], w_qkv[:, 1024:1152]], 1)
    second_cols = jnp.concatenate([w_qkv[:, 512:1024], w_qkv[:, 1152:]], 1)
    mine = jnp.where(first, first_cols, second_cols)
    theirs = core_mate(jnp.where(first, second_cols, first_cols))
    low = jnp.where(first, mine, theirs)
    high = jnp.where(first, theirs, mine)
    unit = jnp.concatenate([low, high], 0)

    place = lambda dx, dy: ((x_hi + dx) % 2) * 4 + (y + dy) % 4
    scalars = jnp.stack(
        [place(1, 2), core, slot, place(0, 0), place(0, 1), place(0, 3), place(0, 2),
         place(1, 0), place(1, 1), place(1, 3)]
    ).astype(jnp.int32)

    ids = jnp.arange(16, dtype=jnp.int32)
    below = jnp.sum((segment_ids[:, :, None] < ids).astype(jnp.int32), 1)
    below = lax.all_to_all(
        jnp.broadcast_to(below[None], (16, 2, 16)), "fsdp", 0, 0, tiled=True
    )
    mate_ids = core_mate(segment_ids)
    both = [segment_ids[0:1], mate_ids[0:1], segment_ids[1:2], mate_ids[1:2]]
    tokens = jnp.concatenate(both, 1)
    queries = jnp.concatenate([segment_ids, mate_ids, segment_ids, mate_ids], 1)

    table = (segment_ids[..., None] == jnp.arange(SEGS, dtype=jnp.int32)).astype(F32)
    per_token = jnp.sum(table * advantages.astype(F32)[:, None, :], -1)
    factor = jnp.float32(2 * 16 * SEQ) / token_count[0].astype(F32)
    cotangent = (upstream.astype(F32) * (per_token * factor)[..., None]).astype(BF16)
    mine_cot = jnp.where(first, cotangent[..., :QCOLS], cotangent[..., QCOLS:])
    other_cot = core_mate(jnp.where(first, cotangent[..., QCOLS:], cotangent[..., :QCOLS]))
    cot = jnp.stack([mine_cot, other_cot], 1)

    rows = [hidden, core_mate(hidden)]
    y1, y3, x0 = from_y(unit, 1), from_y(unit, 3), from_near_x(unit)
    tables = positions(below, tokens, queries, scalars)
    y1, y3, x0 = lax.optimization_barrier((y1, y3, x0))
    y2, x1, x3 = from_y(y1, 1), from_near_x(y1), from_y(x0, 3)
    y2, x1, x3, tables, cot = lax.optimization_barrier((y2, x1, x3, tables, cot))
    cosine_flat, sine_flat, lanes = tables
    cosine = cosine_flat.reshape(2, 2, TOK, HD)
    sine = sine_flat.reshape(2, 2, TOK, HD)
    x2_a, x2_b = from_y(x1[: UNIT // 2], 1), from_y(x3[UNIT // 2 :], 3)
    total = project(rows, [unit, y1, y3, x0], [3, 4, 5, 7], scalars, None)
    total = project(rows, [y2, x1, x3], [6, 8, 9], scalars, total)
    x2_a, x2_b, total = lax.optimization_barrier((x2_a, x2_b, total))
    q, kv, send = project_last(
        rows, [x2_a, x2_b], total, cosine_flat, sine_flat, norm_gains, scalars
    )

    moved = mirror(take(hidden, slot))
    own_rows = jnp.stack([take(hidden, 1 - slot), moved])
    near = lax.dynamic_slice_in_dim(own_rows, (1 - x_hi) * 4 * UNIT, 4 * UNIT, 2)
    near = from_x(after(near, x2_a, x2_b))
    blocks = []
    for step in (0, 1, 3, 2):
        to = (y - step) % 4
        blocks.append(
            jnp.stack(
                [
                    lax.dynamic_slice_in_dim(own_rows, (x_hi * 4 + to) * UNIT, UNIT, 2),
                    lax.dynamic_slice_in_dim(near, to * UNIT, UNIT, 2),
                ]
            )
        )

    gathered = chips_exchange(send)
    gathered, blocks = lax.optimization_barrier((gathered, blocks))
    blocks = [blocks[0], from_y(blocks[1], 1), from_y(blocks[2], 3), from_y(blocks[3], 2)]
    kv_shape = (CHIPS, 2, 2, TOK, HD)
    kv_other = core_mate(gathered).reshape(kv_shape)
    kv_mine = gathered.reshape(kv_shape)

    def attend(moved):
        return attention(
            q.reshape(2, 2, TOK, QCOLS), cot, kv_mine, kv_other, lanes, cosine, sine, norm_gains,
            scalars, moved,
        )

    gp_moved, gain_moved, moved_mine, moved_other = attend(True)
    gp_kept, gain_kept, kept_mine, kept_other = attend(False)
    kept_other, blocks, gp_moved = lax.optimization_barrier(
        (kept_other, blocks, mirror(gp_moved))
    )
    gp_q = jnp.concatenate([gp_kept, gp_moved], 0).reshape(4 * TOK, QCOLS)

    summed = jnp.stack(
        [
            moved_mine.astype(F32) + core_mate(moved_other).astype(F32),
            kept_mine.astype(F32) + core_mate(kept_other).astype(F32),
        ],
        1,
    ).astype(BF16)
    terms = chips_exchange(summed.reshape(CHIPS, 2, 2 * TOK, HD))
    near_q = gather_near(gp_q)
    parts_q = gather_far(gp_q, near_q)
    gp_kv = kv_back(
        terms, kv, cosine_flat, sine_flat, norm_gains, (gain_moved, gain_kept), scalars
    )
    gp_kv = jnp.concatenate([gp_kv[1], mirror(gp_kv[0])], 0)
    gp_kv = after(gp_kv, [part[0][0] for part in parts_q[:7]])
    parts_kv = chips_exchange(jnp.broadcast_to(gp_kv[None], (CHIPS, 4 * TOK + 32, HD)))

    pieces = [
        (3, unit), (4, y1), (5, y3), (6, y2), (7, x0), (8, x1), (9, x3), (0, x2_a, x2_b),
    ]
    keep, give = hidden_grad(gp_q, gp_kv, pieces, scalars)
    grad_hidden = (keep + core_mate(give).astype(F32)).astype(BF16).reshape(hidden.shape)

    features = blocks + [core_mate(b) for b in blocks]
    q_mine, q_give = weight_grad(features, parts_q, QCOLS, scalars, False)
    kv_mine, kv_give, gains = weight_grad(
        features, [[(parts_kv, None)]] * CHIPS, HD, scalars, True
    )
    q_got = core_mate(q_give)
    kv_got = core_mate(kv_give)
    grad_weight = jnp.concatenate(
        [
            jnp.where(first, q_mine, q_got), jnp.where(first, q_got, q_mine),
            jnp.where(first, kv_mine, kv_got), jnp.where(first, kv_got, kv_mine),
        ],
        1,
    )
    grad_gains = (gains + core_mate(gains))[:2]
    return (grad_hidden, grad_weight[None], grad_gains[None])


def solution(mesh):
    in_specs = (
        P("dp", "fsdp", None),
        P("fsdp", None),
        P(),
        P("dp", "fsdp", None),
        P("dp", "fsdp"),
        P("dp", None),
        P(),
        P(),
    )
    out_specs = (P("dp", "fsdp", None), P("dp", "fsdp", None), P("dp", None, None))
    return jax.shard_map(
        per_device, mesh=mesh, in_specs=in_specs, out_specs=out_specs, check_vma=False
    )
```

```python
import math

import jax
import jax.numpy as jnp
from jax import lax
from jax.experimental import pallas as pl
from jax.experimental.pallas import tpu as pltpu
from jax.sharding import PartitionSpec as P

HD = 128
HEADS = 4
TOK = 96
CHIPS = 8
UNIT = 640
HALF_COLS = 640
QCOLS = HEADS * HD
SEQ = 1536
SEGS = 8
EPSILON = 1e-06
THETA_LOG = math.log(1000000.0)
SCALING = 1.0 / math.sqrt(HD)
EXP2_SCALE = SCALING * math.log2(math.e)
F32 = jnp.float32
BF16 = jnp.bfloat16
NN = (((1,), (0,)), ((), ()))
NT = (((1,), (1,)), ((), ()))
TN = (((0,), (0,)), ((), ()))
VMEM_LIMIT = 56 * 1024 * 1024


def core_mate(array):
    return lax.ppermute(array, "fsdp", [(i, i ^ 1) for i in range(16)])


def from_y(array, step):
    def there(i):
        return (i & 8) | (((i // 2 - step) % 4) * 2) | (i & 1)

    return lax.ppermute(array, "fsdp", [(i, there(i)) for i in range(16)])


def from_x(array):
    return lax.ppermute(array, "fsdp", [(i, i ^ 8) for i in range(16)])


def from_near_x(array):
    pairs = [(d * 16 + i, (d ^ 8) * 16 + (i ^ 8)) for d in range(16) for i in range(16)]
    return lax.ppermute(array, ("dp", "fsdp"), pairs)


def mirror(array):
    return lax.ppermute(array, "dp", [(i, 15 - i) for i in range(16)])


def chips_exchange(blocks):
    return lax.all_to_all(
        blocks, "fsdp", 0, 0, tiled=True,
        axis_index_groups=[list(range(0, 16, 2)), list(range(1, 16, 2))],
    )


def after(array, *others):
    return lax.optimization_barrier((array, others))[0]


def dot(left, right, dims):
    return lax.dot_general(left, right, dims, preferred_element_type=F32)


def call(kernel, out_shape, arrays, flops, scalars=None, grid=(1,), in_specs=None, out_specs=None,
         scratch=(), name=None):
    whole = lambda s: pl.BlockSpec(s.shape, lambda *_, n=len(s.shape): (0,) * n)
    in_specs = in_specs or [whole(a) for a in arrays]
    outs = out_shape if isinstance(out_shape, (list, tuple)) else [out_shape]
    out_specs = out_specs or [whole(s) for s in outs]
    return pl.pallas_call(
        kernel,
        out_shape=list(outs),
        grid_spec=pltpu.PrefetchScalarGridSpec(
            num_scalar_prefetch=1, grid=grid, in_specs=in_specs, out_specs=out_specs,
            scratch_shapes=list(scratch),
        ),
        compiler_params=pltpu.CompilerParams(vmem_limit_bytes=VMEM_LIMIT),
        cost_estimate=pl.CostEstimate(flops=flops, bytes_accessed=0, transcendentals=0),
        name=name,
    )(scalars, *arrays)


def block_of(place):
    return pl.BlockSpec((2, TOK, UNIT), lambda i, s, j=place: (0, 0, s[j]))


def joined(own, other):
    return jnp.concatenate([own[0], other[0], own[1], other[1]], 0)


def whole_spec(a):
    return pl.BlockSpec(a.shape, lambda *_, n=len(a.shape): (0,) * n)


def project(rows, units, places, scalars, total):
    n = len(units)

    def kernel(s_ref, *refs):
        acc = refs[3 * n][...] if total is not None else None
        for j in range(n):
            term = dot(joined(refs[2 * j], refs[2 * j + 1]), refs[2 * n + j][...], NN)
            acc = term if acc is None else acc + term
        refs[-1][...] = acc

    extra = [] if total is None else [total]
    return call(
        kernel, jax.ShapeDtypeStruct((4 * TOK, HALF_COLS), F32),
        list(rows) * n + units + extra, 0, scalars,
        in_specs=[block_of(j) for j in places for _ in rows]
        + [whole_spec(a) for a in units + extra],
        name="project",
    )[0]


def rotated(x, cosine, sine):
    return x * cosine + pltpu.roll(x, HD // 2, 1) * sine


def unrotated(y, cosine, sine):
    return y * cosine - pltpu.roll(y, HD // 2, 1) * sine


def inverse_rms(x):
    return lax.rsqrt(jnp.mean(x * x, -1, keepdims=True) + EPSILON)


def swap_cores(x):
    return jnp.concatenate([x[i * TOK : (i + 1) * TOK] for i in (1, 0, 3, 2)], 0)


def project_last(rows, unit, total, cosine, sine, gains, scalars):
    def kernel(s_ref, own_ref, other_ref, low_ref, high_ref, total_ref, cos_ref, sin_ref,
               gain_ref, q_ref, kv_ref, send_ref):
        right = jnp.concatenate([low_ref[...], high_ref[...]], 0)
        acc = total_ref[...] + dot(joined(own_ref, other_ref), right, NN)
        q_ref[...] = acc[:, :QCOLS]
        x = acc[:, QCOLS:]
        kv_ref[...] = x

        @pl.when(s_ref[1] == 0)
        def _():
            kn = x * inverse_rms(x) * gain_ref[1:2, :]
            kr = rotated(kn, cos_ref[...], sin_ref[...]).astype(BF16)
            for i in range(CHIPS):
                send_ref[i] = kr

        @pl.when(s_ref[1] != 0)
        def _():
            v = swap_cores(x.astype(BF16))
            for i in range(CHIPS):
                send_ref[i] = v

    arrays = [*rows, *unit, total, cosine, sine, gains]
    shapes = [
        jax.ShapeDtypeStruct((4 * TOK, QCOLS), F32),
        jax.ShapeDtypeStruct((4 * TOK, HD), F32),
        jax.ShapeDtypeStruct((CHIPS, 4 * TOK, HD), BF16),
    ]
    return call(
        kernel, shapes, arrays, 4 * 10**8, scalars,
        in_specs=[block_of(0)] * 2 + [whole_spec(a) for a in arrays[2:]], name="project_last",
    )


def positions(below, tokens, queries, scalars):
    count = 4 * TOK

    def kernel(s_ref, below_ref, tokens_ref, queries_ref, cos_ref, sin_ref, out_ref):
        counts = jnp.sum(below_ref[...], 0)
        lane = lax.broadcasted_iota(jnp.int32, (1, count), 1)
        shard = 2 * s_ref[3] + s_ref[1]
        mate = 2 * s_ref[3] + 1 - s_ref[1]
        slot = jnp.where((lane // TOK) % 2 == 0, shard, mate) * TOK + lane % TOK

        def start_of(seg, pack):
            start = jnp.zeros(seg.shape, jnp.int32)
            for k in range(1, SEGS + 1):
                start = jnp.where(seg == k, counts[pack : pack + 1, k : k + 1], start)
            return start

        seg = tokens_ref[...]
        start = jnp.where(lane < 2 * TOK, start_of(seg, 0), start_of(seg, 1))
        place = jnp.broadcast_to((slot - start).astype(F32), (8, count))
        for p in range(2):
            out_ref[p] = jnp.broadcast_to(slot, (8, count))
            out_ref[p, 0:1, :] = start_of(queries_ref[p : p + 1, :], p)
        half = lax.broadcasted_iota(jnp.int32, (1, HD), 1)
        inverse = jnp.exp(-((half % (HD // 2)).astype(F32) * (2.0 / HD)) * THETA_LOG)
        angles = place.T[:, 0:1] * inverse
        cos_ref[...] = jnp.cos(angles)
        sin_ref[...] = jnp.sin(angles) * jnp.where(half < HD // 2, -1.0, 1.0)

    table = jax.ShapeDtypeStruct((count, HD), F32)
    return call(
        kernel, [table, table, jax.ShapeDtypeStruct((2, 8, count), jnp.int32)],
        [below, tokens, queries], 0, scalars, name="positions",
    )


def attention(q, cotangent, kv_a, kv_b, rows, cosine, sine, gains, scalars, moved):
    chips = 2
    chunk = chips * 2 * TOK
    lanes = HEADS * 2 * TOK
    queries = 2 * TOK

    def kernel(s_ref, q_ref, c_ref, a_ref, b_ref, rows_ref, cos_ref, sin_ref, gain_ref,
               gp_ref, gg_ref, mine_ref, other_ref, k_s, v_s, e_s, d_s):
        first = s_ref[1] == 0

        @pl.when(first)
        def _():
            k_s[...] = a_ref[...].reshape(SEQ, HD)
            v_s[...] = b_ref[...].reshape(SEQ, HD)

        @pl.when(jnp.logical_not(first))
        def _():
            k_s[...] = b_ref[...].reshape(SEQ, HD)
            v_s[...] = a_ref[...].reshape(SEQ, HD)

        cos = cos_ref[...].reshape(queries, HD)
        sin = sin_ref[...].reshape(queries, HD)
        gain = gain_ref[0:1, :]
        q_all = q_ref[...].reshape(queries, QCOLS)
        c_all = c_ref[...].reshape(queries, QCOLS)
        xs = [q_all[:, h * HD : (h + 1) * HD] for h in range(HEADS)]
        rms = [inverse_rms(x) for x in xs]
        qs = jnp.concatenate(
            [rotated(x * r * gain, cos, sin).astype(BF16) for x, r in zip(xs, rms)], 0
        )
        cs = jnp.concatenate([c_all[:, h * HD : (h + 1) * HD] for h in range(HEADS)], 0)
        half = lanes // 2
        start = rows_ref[0, 0:1, :half]
        place = rows_ref[0, 1:2, :half]
        total = jnp.zeros((1, lanes), F32)
        inner = jnp.zeros((1, lanes), F32)
        for c in range(SEQ // chunk):
            at = pl.ds(c * chunk, chunk)
            scores = dot(k_s[at, :], qs, NT)
            u = lax.broadcasted_iota(jnp.int32, (chunk, half), 0) + c * chunk
            seen = jnp.where((u >= start) & (u <= place), 1.0, 0.0)
            e = jnp.exp2(scores * EXP2_SCALE) * jnp.concatenate([seen, seen], 1)
            d = dot(v_s[at, :], cs, NT)
            total = total + jnp.sum(e, 0, keepdims=True)
            inner = inner + jnp.sum(e * d, 0, keepdims=True)
            e_s[at, :] = e
            d_s[at, :] = d
        inverse = 1.0 / total
        inner = inner * inverse
        grad_t = jnp.zeros((HD, lanes), F32)
        for c in range(SEQ // chunk):
            at = pl.ds(c * chunk, chunk)
            p = e_s[at, :] * inverse
            ds = (p * (d_s[at, :] - inner)).astype(BF16)
            dv = dot(p.astype(BF16), cs, NN).astype(BF16).reshape(chips, 2, TOK, HD)
            dk = (dot(ds, qs, NN) * SCALING).astype(BF16).reshape(chips, 2, TOK, HD)
            grad_t = grad_t + dot(k_s[at, :], ds, TN)
            own = pl.ds(c * chips, chips)

            @pl.when(first)
            def _():
                mine_ref[own] = dk
                other_ref[own] = dv

            @pl.when(jnp.logical_not(first))
            def _():
                mine_ref[own] = dv
                other_ref[own] = dk

        grad = grad_t.T * SCALING
        outs = []
        gain_sum = jnp.zeros((1, HD), F32)
        for h in range(HEADS):
            y = unrotated(grad[h * queries : (h + 1) * queries], cos, sin)
            x, r = xs[h], rms[h]
            weighted = y * gain
            mean = jnp.mean(x * weighted, -1, keepdims=True)
            outs.append((r * weighted - x * (r * r * r) * mean).astype(BF16))
            gain_sum = gain_sum + jnp.sum(y * (x * r), 0, keepdims=True)
        gp_ref[...] = jnp.concatenate(outs, 1).reshape(2, TOK, QCOLS)
        gg_ref[...] = jnp.broadcast_to(gain_sum, (8, HD))

    pack = lambda s: s[2] if moved else 1 - s[2]
    token_spec = lambda cols: pl.BlockSpec((1, 2, TOK, cols), lambda i, s: (pack(s), 0, 0, 0))
    kv_spec = pl.BlockSpec((CHIPS, 1, 2, TOK, HD), lambda i, s: (0, pack(s), 0, 0, 0))
    shapes = [
        jax.ShapeDtypeStruct((2, TOK, QCOLS), BF16),
        jax.ShapeDtypeStruct((8, HD), F32),
        jax.ShapeDtypeStruct((CHIPS, 2, TOK, HD), BF16),
        jax.ShapeDtypeStruct((CHIPS, 2, TOK, HD), BF16),
    ]
    return call(
        kernel, shapes, [q, cotangent, kv_a, kv_b, rows, cosine, sine, gains],
        2 * 5 * 2 * SEQ * lanes * HD, scalars,
        in_specs=[
            token_spec(QCOLS), token_spec(QCOLS), kv_spec, kv_spec,
            pl.BlockSpec((1, 8, lanes // 2), lambda i, s: (pack(s), 0, 0)),
            token_spec(HD), token_spec(HD), whole_spec(gains),
        ],
        scratch=[
            pltpu.VMEM((SEQ, HD), BF16), pltpu.VMEM((SEQ, HD), BF16),
            pltpu.VMEM((SEQ, lanes), F32), pltpu.VMEM((SEQ, lanes), F32),
        ],
        name="attention",
    )


def kv_back(terms, kv, cosine, sine, gains, gain_parts, scalars):
    rows = 2 * TOK

    def kernel(s_ref, t_ref, kv_ref, cos_ref, sin_ref, gain_ref, moved_ref, kept_ref, out_ref):
        grad = t_ref[0, 0].astype(F32)
        for i in range(1, CHIPS):
            grad = grad + t_ref[i, 0].astype(F32)
        q_sum = jnp.where(pl.program_id(0) == 0, moved_ref[0:1, :], kept_ref[0:1, :])

        def put(values, key_sum):
            parts = []
            for s in (q_sum, key_sum):
                high = s.astype(BF16)
                rest = s - high.astype(F32)
                middle = rest.astype(BF16)
                parts += [high.astype(F32), middle.astype(F32), rest - middle.astype(F32)]
            parts.append(jnp.zeros((16 - len(parts), HD), F32))
            out_ref[0, :rows, :] = values
            out_ref[0, rows:, :] = jnp.concatenate(parts, 0).astype(BF16)

        @pl.when(s_ref[1] == 0)
        def _():
            y = unrotated(grad, cos_ref[...], sin_ref[...])
            x = kv_ref[...]
            r = inverse_rms(x)
            weighted = y * gain_ref[1:2, :]
            mean = jnp.mean(x * weighted, -1, keepdims=True)
            values = (r * weighted - x * (r * r * r) * mean).astype(BF16)
            put(values, jnp.sum(y * (x * r), 0, keepdims=True))

        @pl.when(s_ref[1] != 0)
        def _():
            values = grad.astype(BF16)
            put(jnp.concatenate([values[TOK:], values[:TOK]], 0), jnp.zeros((1, HD), F32))

    pack_spec = pl.BlockSpec((rows, HD), lambda p, s: (s[2] + p - 2 * s[2] * p, 0))
    arrays = [terms, kv, cosine, sine, gains, *gain_parts]
    return call(
        kernel, jax.ShapeDtypeStruct((2, rows + 16, HD), BF16), arrays, 0, scalars, grid=(2,),
        in_specs=[pl.BlockSpec((CHIPS, 1, rows, HD), lambda p, s: (0, p, 0, 0))]
        + [pack_spec] * 3 + [whole_spec(a) for a in arrays[4:]],
        out_specs=[pl.BlockSpec((1, rows + 16, HD), lambda p, s: (p, 0, 0))],
        name="kv_back",
    )[0]


def hidden_grad(left, units, place, width, scalars, name):
    def kernel(s_ref, left_ref, *refs):
        keep_ref, send_ref = refs[-2:]
        refs = list(refs)
        for where, *pieces in units:
            col = pl.multiple_of(s_ref[where] * UNIT, 128)
            unit = jnp.concatenate([refs.pop(0)[...] for _ in pieces], 0)
            out = dot(left_ref[...], unit, NT)
            for i in range(2):
                slot = s_ref[2] if i else 1 - s_ref[2]
                at = (pl.ds(pl.multiple_of(slot * TOK, TOK), TOK), pl.ds(col, UNIT))
                keep_ref[at] = out[2 * i * TOK : (2 * i + 1) * TOK]
                send_ref[at] = out[(2 * i + 1) * TOK : (2 * i + 2) * TOK].astype(BF16)

    shapes = [
        jax.ShapeDtypeStruct((2 * TOK, CHIPS * UNIT), F32),
        jax.ShapeDtypeStruct((2 * TOK, CHIPS * UNIT), BF16),
    ]
    pieces = [p for u in units for p in u[1:]]
    return call(
        kernel, shapes, [left] + pieces, 10**9, scalars,
        in_specs=[whole_spec(left)]
        + [pl.BlockSpec((p.shape[0], width), lambda i, s: (0, place)) for p in pieces],
        name=name,
    )


def weight_grad(features, parts, cols, scalars, with_gains):
    arrays, index = [], []
    for part in parts:
        for a, at in part:
            if not any(a is b for b in arrays):
                arrays.append(a)
        index.append([(next(i for i, b in enumerate(arrays) if a is b), at) for a, at in part])

    def kernel(s_ref, *refs):
        places = (3, 4, 5, 6, 7, 8, 9, 0)
        feature_refs, refs = refs[:8], refs[8:]
        acc = refs[-1]
        total = None
        gains = None
        for j in range(0, CHIPS, 2):
            left, right = [], []
            for i in (j, j + 1):
                own, other = feature_refs[i % 4], feature_refs[4 + i % 4]
                left += [f[i // 4, pack] for pack in range(2) for f in (own, other)]
                rows = [refs[a][s_ref[places[i]] if at is None else at] for a, at in index[i]]
                if with_gains:
                    half = 2 * TOK + 16
                    part = rows[0][half - 16 : half].astype(F32)
                    part = part + rows[0][2 * half - 16 :].astype(F32)
                    gains = part if gains is None else gains + part
                    rows = [rows[0][: half - 16], rows[0][half : 2 * half - 16]]
                right += rows
            left, right = jnp.concatenate(left, 0), jnp.concatenate(right, 0)
            if with_gains:
                term = dot(right, left, TN)
                total = term if total is None else total + term
            elif j == 0:
                acc[...] = dot(left, right, TN)
            else:
                acc[...] += dot(left, right, TN)
        outs = refs[len(arrays) : -1]
        if with_gains:
            acc[...] = total.T
            q_sum = gains[0:1] + gains[1:2] + gains[2:3]
            k_sum = gains[3:4] + gains[4:5] + gains[5:6]
            outs[2][...] = jnp.concatenate([q_sum, k_sum, jnp.zeros((6, HD), F32)], 0)
        core = s_ref[1]
        rows = UNIT // 2
        outs[0][...] = acc[pl.ds(pl.multiple_of(core * rows, rows), rows), :]
        outs[1][...] = acc[pl.ds(pl.multiple_of((1 - core) * rows, rows), rows), :]

    shape = jax.ShapeDtypeStruct((UNIT // 2, cols), F32)
    shapes = [shape, shape]
    if with_gains:
        shapes.append(jax.ShapeDtypeStruct((8, HD), F32))
    return call(
        kernel, shapes, [*features] + arrays, 4 * 10**10 if with_gains else 3 * 10**9, scalars,
        scratch=[pltpu.VMEM((UNIT, cols), F32)],
        name="weight_grad_kv" if with_gains else "weight_grad_q",
    )


def gather_near(unit):
    return from_y(unit, 1), from_y(unit, 3), from_x(unit)


def gather_far(unit, near):
    y1, y3, x0 = near
    y2 = from_y(y1, 1)
    x1 = from_y(x0, 1)
    x3 = from_y(x0, 3)
    cut = 2 * TOK
    x2 = [from_y(x1[:cut], 1), from_y(x3[cut:], 3)]
    parts = [[(u, slice(None))] for u in (unit, y1, y3, y2, x0, x1, x3)]
    return parts + [[(u, slice(None)) for u in x2]]


def per_device(
    hidden, w_qkv, norm_gains, upstream, segment_ids, advantages, swap_slot, token_count
):
    data_rank = lax.axis_index("dp")
    shard = lax.axis_index("fsdp")
    core = shard % 2
    chip = shard // 2
    y = chip % 4
    x_hi = chip // 4
    first = core == 0
    slot = swap_slot[jnp.minimum(data_rank, 15 - data_rank)]

    def take(array, index):
        return lax.dynamic_index_in_dim(array, index, 0, keepdims=False)

    first_cols = jnp.concatenate([w_qkv[:, :512], w_qkv[:, 1024:1152]], 1)
    second_cols = jnp.concatenate([w_qkv[:, 512:1024], w_qkv[:, 1152:]], 1)
    mine = jnp.where(first, first_cols, second_cols)
    theirs = core_mate(jnp.where(first, second_cols, first_cols))
    low = jnp.where(first, mine, theirs)
    high = jnp.where(first, theirs, mine)
    unit = jnp.concatenate([low, high], 0)

    place = lambda dx, dy: ((x_hi + dx) % 2) * 4 + (y + dy) % 4
    scalars = jnp.stack(
        [place(1, 2), core, slot, place(0, 0), place(0, 1), place(0, 3), place(0, 2),
         place(1, 0), place(1, 1), place(1, 3)]
    ).astype(jnp.int32)

    ids = jnp.arange(16, dtype=jnp.int32)
    below = jnp.sum((segment_ids[:, :, None] < ids).astype(jnp.int32), 1)
    below = lax.all_to_all(
        jnp.broadcast_to(below[None], (16, 2, 16)), "fsdp", 0, 0, tiled=True
    )
    mate_ids = core_mate(segment_ids)
    both = [segment_ids[0:1], mate_ids[0:1], segment_ids[1:2], mate_ids[1:2]]
    tokens = jnp.concatenate(both, 1)
    queries = jnp.concatenate([segment_ids, mate_ids, segment_ids, mate_ids], 1)

    table = (segment_ids[..., None] == jnp.arange(SEGS, dtype=jnp.int32)).astype(F32)
    per_token = jnp.sum(table * advantages.astype(F32)[:, None, :], -1)
    factor = jnp.float32(2 * 16 * SEQ) / token_count[0].astype(F32)
    cotangent = (upstream.astype(F32) * (per_token * factor)[..., None]).astype(BF16)
    mine_cot = jnp.where(first, cotangent[..., :QCOLS], cotangent[..., QCOLS:])
    other_cot = core_mate(jnp.where(first, cotangent[..., QCOLS:], cotangent[..., :QCOLS]))
    cot = jnp.stack([mine_cot, other_cot], 1)

    rows = [hidden, core_mate(hidden)]
    y1, y3, x0 = from_y(unit, 1), from_y(unit, 3), from_near_x(unit)
    tables = positions(below, tokens, queries, scalars)
    y1, y3, x0 = lax.optimization_barrier((y1, y3, x0))
    y2, x1, x3 = from_y(y1, 1), from_near_x(y1), from_y(x0, 3)
    y2, x1, x3, tables, cot = lax.optimization_barrier((y2, x1, x3, tables, cot))
    cosine_flat, sine_flat, lanes = tables
    cosine = cosine_flat.reshape(2, 2, TOK, HD)
    sine = sine_flat.reshape(2, 2, TOK, HD)
    x2_a, x2_b = from_y(x1[: UNIT // 2], 1), from_y(x3[UNIT // 2 :], 3)
    total = project(rows, [unit, y1, y3, x0], [3, 4, 5, 7], scalars, None)
    total = project(rows, [y2, x1, x3], [6, 8, 9], scalars, total)
    x2_a, x2_b, total = lax.optimization_barrier((x2_a, x2_b, total))
    q, kv, send = project_last(
        rows, [x2_a, x2_b], total, cosine_flat, sine_flat, norm_gains, scalars
    )

    moved = mirror(take(hidden, slot))
    own_rows = jnp.stack([take(hidden, 1 - slot), moved])
    near = lax.dynamic_slice_in_dim(own_rows, (1 - x_hi) * 4 * UNIT, 4 * UNIT, 2)
    near = from_x(after(near, y2, x1, x3))
    blocks = []
    for step in (0, 1, 3, 2):
        to = (y - step) % 4
        blocks.append(
            jnp.stack(
                [
                    lax.dynamic_slice_in_dim(own_rows, (x_hi * 4 + to) * UNIT, UNIT, 2),
                    lax.dynamic_slice_in_dim(near, to * UNIT, UNIT, 2),
                ]
            )
        )

    gathered = chips_exchange(send)
    gathered, blocks = lax.optimization_barrier((gathered, blocks))
    blocks = [blocks[0], from_y(blocks[1], 1), from_y(blocks[2], 3), from_y(blocks[3], 2)]
    kv_shape = (CHIPS, 2, 2, TOK, HD)
    kv_other = core_mate(gathered).reshape(kv_shape)
    kv_mine = gathered.reshape(kv_shape)

    def attend(moved):
        return attention(
            q.reshape(2, 2, TOK, QCOLS), cot, kv_mine, kv_other, lanes, cosine, sine, norm_gains,
            scalars, moved,
        )

    gp_moved, gain_moved, moved_mine, moved_other = attend(True)
    gp_kept, gain_kept, kept_mine, kept_other = attend(False)
    kept_other, blocks, gp_moved = lax.optimization_barrier(
        (kept_other, blocks, mirror(gp_moved))
    )
    gp_q = jnp.concatenate([gp_kept, gp_moved], 0).reshape(4 * TOK, QCOLS)

    summed = jnp.stack(
        [
            moved_mine.astype(F32) + core_mate(moved_other).astype(F32),
            kept_mine.astype(F32) + core_mate(kept_other).astype(F32),
        ],
        1,
    ).astype(BF16)
    terms = chips_exchange(summed.reshape(CHIPS, 2, 2 * TOK, HD))
    near_q = gather_near(gp_q)
    pieces = [
        (3, unit), (4, y1), (5, y3), (6, y2), (7, x0), (8, x1), (9, x3), (0, x2_a, x2_b),
    ]
    keep_q, give_q = hidden_grad(gp_q, pieces, 0, QCOLS, scalars, "hidden_grad_q")
    terms, keep_q, give_q = lax.optimization_barrier((terms, keep_q, give_q))
    parts_q = gather_far(gp_q, near_q)
    gp_kv = kv_back(
        terms, kv, cosine_flat, sine_flat, norm_gains, (gain_moved, gain_kept), scalars
    )
    gp_kv = jnp.concatenate([gp_kv[1], mirror(gp_kv[0])], 0)
    gp_kv = after(gp_kv, [part[0][0] for part in parts_q[:7]])
    parts_kv = chips_exchange(jnp.broadcast_to(gp_kv[None], (CHIPS, 4 * TOK + 32, HD)))

    gp_keys = jnp.concatenate([gp_kv[: 2 * TOK], gp_kv[2 * TOK + 16 : 4 * TOK + 16]], 0)
    keep, give = hidden_grad(gp_keys, pieces, QCOLS // HD, HD, scalars, "hidden_grad_kv")
    grad_hidden = keep_q + core_mate(give_q).astype(F32) + keep + core_mate(give).astype(F32)
    grad_hidden = grad_hidden.astype(BF16).reshape(hidden.shape)

    features = blocks + [core_mate(b) for b in blocks]
    q_mine, q_give = weight_grad(features, parts_q, QCOLS, scalars, False)
    kv_mine, kv_give, gains = weight_grad(
        features, [[(parts_kv, None)]] * CHIPS, HD, scalars, True
    )
    q_got = core_mate(q_give)
    kv_got = core_mate(kv_give)
    grad_weight = jnp.concatenate(
        [
            jnp.where(first, q_mine, q_got), jnp.where(first, q_got, q_mine),
            jnp.where(first, kv_mine, kv_got), jnp.where(first, kv_got, kv_mine),
        ],
        1,
    )
    grad_gains = (gains + core_mate(gains))[:2]
    return (grad_hidden, grad_weight[None], grad_gains[None])


def solution(mesh):
    in_specs = (
        P("dp", "fsdp", None),
        P("fsdp", None),
        P(),
        P("dp", "fsdp", None),
        P("dp", "fsdp"),
        P("dp", None),
        P(),
        P(),
    )
    out_specs = (P("dp", "fsdp", None), P("dp", "fsdp", None), P("dp", None, None))
    return jax.shard_map(
        per_device, mesh=mesh, in_specs=in_specs, out_specs=out_specs, check_vma=False
    )
```
